256 devices in a mesh: dp: 16 (over x, z_lo, core), section: 4 (over z_hi), tensor: 4 (over y).
Axes of the slice: x: 4, y: 4, z: 8 (z_hi: 4, z_lo: 2; z = z_hi * 2 + z_lo), core: 2. Of those that a mesh axis runs over, the one named last changes fastest.
Arguments:
- down_input: bfloat16 [2, 128, 4096], P(None, None, 'tensor'), may hold values from -6 to 6
- up_input: bfloat16 [2, 128, 4096], P(None, None, 'tensor'), may hold values from -6 to 6
- down_gain: bfloat16 [4, 4096], P('section', 'tensor'), may hold values from 0.099609375 to 1.8984375
- down_gate: bfloat16 [4, 4096, 12288], P('section', 'tensor', 'dp'), may hold values from -0.09375 to 0.09375
- down_up: bfloat16 [4, 4096, 12288], P('section', 'tensor', 'dp'), may hold values from -0.09375 to 0.09375
- down_proj: bfloat16 [4, 12288, 4096], P('section', 'dp', 'tensor'), may hold values from -0.0546875 to 0.0546875
- up_gain: bfloat16 [4, 4096], P('section', 'tensor'), may hold values from 0.099609375 to 1.8984375
- up_gate: bfloat16 [4, 4096, 12288], P('section', 'tensor', 'dp'), may hold values from -0.09375 to 0.09375
- up_up: bfloat16 [4, 4096, 12288], P('section', 'tensor', 'dp'), may hold values from -0.09375 to 0.09375
- up_proj: bfloat16 [4, 12288, 4096], P('section', 'dp', 'tensor'), may hold values from -0.0546875 to 0.0546875
Outputs:
- down_acts: bfloat16 [4, 2, 128, 4096], P('section', None, 'dp', 'tensor')
- up_acts: bfloat16 [4, 2, 128, 4096], P('section', None, 'dp', 'tensor')
The draws below stay inside these ranges and needn't reach their ends.
All inputs are finite; a program needn't handle non-finite values.
Results may differ from the reference program's by a relative error of at most 0.035.
Values may be sent and summed in bfloat16 or wider, within the bound.
No kernel may reach another device: no remote copies, remote signals or barrier semaphores. Data moves between devices by JAX's collectives and lax.ppermute only.
A program may use at most 64 MiB of HBM per device.

```python
import jax
import jax.numpy as jnp
from jax import lax

D = 4096
FF = 12288
MB_TOK = 128
MBS = 2
N_SECTION = 4
N_TENSOR = 4


def block_scale(stream_key, extent, split, least, top_value):
    factor_of = 1.0
    for dim, parts in split:
        steps = jax.random.uniform(jax.random.fold_in(jax.random.fold_in(stream_key, 6), dim), (parts,), jnp.float32, least / len(split), top_value / len(split))
        factor_of = factor_of * jnp.repeat(jnp.exp(steps), extent[dim] // parts).reshape((-1,) + (1,) * (len(extent) - 1 - dim))
    return factor_of


def scatter_about(stream_key, extent, width, reach, split=(), kind=jnp.bfloat16):
    values = width * jax.random.normal(stream_key, extent, jnp.float32)
    if split:
        values = values * block_scale(stream_key, extent, split, -0.22, 0.18)
    return jnp.clip(values, -reach, reach).astype(kind)


def setup_inputs(seed: int = 0) -> dict:
    splits = jax.random.split(jax.random.key(seed), 11)
    down_input = scatter_about(splits[0], (MBS, MB_TOK, D), 1.0, 6.0, ((2, 4),))
    up_input = scatter_about(splits[1], (MBS, MB_TOK, D), 1.0, 6.0, ((2, 4),))
    down_gain = jnp.clip(1.0 + 0.18 * jax.random.normal(splits[2], (N_SECTION, D), jnp.float32), 0.099609375, 1.8984375).astype(jnp.bfloat16)
    down_gate = scatter_about(splits[3], (N_SECTION, D, FF), D ** -0.5, 0.09375, ((0, 4), (1, 4), (2, 16)))
    down_up = scatter_about(splits[4], (N_SECTION, D, FF), D ** -0.5, 0.09375, ((0, 4), (1, 4), (2, 16)))
    down_proj = scatter_about(splits[5], (N_SECTION, FF, D), FF ** -0.5, 0.0546875, ((0, 4), (1, 16), (2, 4)))
    up_gain = jnp.clip(1.0 + 0.18 * jax.random.normal(splits[6], (N_SECTION, D), jnp.float32), 0.099609375, 1.8984375).astype(jnp.bfloat16)
    up_gate = scatter_about(splits[7], (N_SECTION, D, FF), D ** -0.5, 0.09375, ((0, 4), (1, 4), (2, 16)))
    up_up = scatter_about(splits[8], (N_SECTION, D, FF), D ** -0.5, 0.09375, ((0, 4), (1, 4), (2, 16)))
    up_proj = scatter_about(splits[9], (N_SECTION, FF, D), FF ** -0.5, 0.0546875, ((0, 4), (1, 16), (2, 4)))
    return {"down_input": down_input, "up_input": up_input, "down_gain": down_gain, "down_gate": down_gate, "down_up": down_up, "down_proj": down_proj, "up_gain": up_gain, "up_gate": up_gate, "up_up": up_up, "up_proj": up_proj}


epsilon = 1e-05

def feed_forward(current, gain_row, gate_matrix, up_matrix, down_matrix):
    widened = current.astype(jnp.float32)
    inverse = lax.rsqrt(lax.optimization_barrier(jnp.mean(widened * widened, axis=1, keepdims=True)) + epsilon)
    normed = (widened * inverse * gain_row.astype(jnp.float32)[None, :]).astype(jnp.bfloat16)
    block_width = D // N_TENSOR
    gate_vals = jnp.zeros((current.shape[0], gate_matrix.shape[1]), jnp.float32)
    up_vals = jnp.zeros((current.shape[0], up_matrix.shape[1]), jnp.float32)
    for block_index in range(N_TENSOR):
        lower = block_index * block_width
        rows_in = normed[:, lower:lower + block_width]
        gate_part = jnp.dot(rows_in, gate_matrix[lower:lower + block_width], preferred_element_type=jnp.float32).astype(jnp.bfloat16)
        up_part = jnp.dot(rows_in, up_matrix[lower:lower + block_width], preferred_element_type=jnp.float32).astype(jnp.bfloat16)
        gate_part, up_part = lax.optimization_barrier((gate_part, up_part))
        gate_vals = gate_vals + gate_part.astype(jnp.float32)
        up_vals = up_vals + up_part.astype(jnp.float32)
    hidden = (jax.nn.silu(gate_vals) * up_vals).astype(jnp.bfloat16)
    branch_total = jnp.dot(hidden, down_matrix, preferred_element_type=jnp.float32)
    return (widened + branch_total).astype(jnp.bfloat16)

def reference(down_input, up_input, down_gain, down_gate, down_up, down_proj, up_gain, up_gate, up_up, up_proj):
    down_results = []
    up_results = []
    for batch_slot in range(MBS):
        current = down_input[batch_slot]
        per_section = []
        for section_index in range(N_SECTION):
            current = feed_forward(current, down_gain[section_index], down_gate[section_index], down_up[section_index], down_proj[section_index])
            per_section.append(current)
        down_results.append(jnp.stack(per_section))
        current = up_input[batch_slot]
        per_section = []
        for section_index in reversed(range(N_SECTION)):
            current = feed_forward(current, up_gain[section_index], up_gate[section_index], up_up[section_index], up_proj[section_index])
            per_section.append(current)
        up_results.append(jnp.stack(per_section[::-1]))
    return (jnp.stack(down_results, axis=1), jnp.stack(up_results, axis=1))
```

```python
import jax
import jax.numpy as jnp
from jax import lax
from jax.experimental import pallas as pl
from jax.experimental.pallas import tpu as pltpu
from jax.sharding import PartitionSpec as P

EPSILON = 1e-05
X, ZL, CORE, TENSOR = 4, 2, 2, 4
VMEM_LIMIT = 48 * 1024 * 1024
f32, bf16 = jnp.float32, jnp.bfloat16


def along(value, axis, pairs):
    return lax.ppermute(value, axis, pairs)


def ring(steps, count):
    return [(i, (i + steps) % count) for i in range(count)]


def x_pairs(steps):
    return [(i, (i + 4 * steps) % 16) for i in range(16)]


CORE_PAIRS = [(i, i ^ 1) for i in range(16)]
ZL_PAIRS = [(i, i ^ 2) for i in range(16)]


def section_pairs(moves, flip):
    return [(d * 4 + a, (d ^ flip) * 4 + b) for d in range(16) for a, b in moves]


MOVES = ([(0, 1), (3, 2)], [(1, 2), (2, 1)], [(2, 3), (1, 0)])


def call(kernel, outs, ins, scratch=(), flops=0, moved=0):
    return pl.pallas_call(
        kernel,
        out_shape=[jax.ShapeDtypeStruct(s, d) for s, d in outs],
        in_specs=ins,
        out_specs=[pl.BlockSpec(memory_space=pltpu.VMEM)] * len(outs),
        scratch_shapes=list(scratch),
        compiler_params=pltpu.CompilerParams(vmem_limit_bytes=VMEM_LIMIT),
        cost_estimate=pl.CostEstimate(flops=flops, bytes_accessed=moved, transcendentals=0),
    )


V = pl.BlockSpec(memory_space=pltpu.VMEM)
A = pl.BlockSpec(memory_space=pl.ANY)


def chosen(early):
    return (lax.axis_index("section") < 2) == early


def fetch(early, pairs, sems):
    down = chosen(early)

    @pl.when(down)
    def _():
        for n, (first, _, target) in enumerate(pairs):
            pltpu.make_async_copy(first, target, sems.at[n]).start()

    @pl.when(jnp.logical_not(down))
    def _():
        for n, (_, second, target) in enumerate(pairs):
            pltpu.make_async_copy(second, target, sems.at[n]).start()


def gate_up(xs, gains, gates, ups, early):
    n = len(xs)
    tokens = sum(x.shape[0] for x in xs)
    depth, width = gates[0].shape[1:]
    count = tokens // TENSOR

    def kernel(*refs):
        x_refs, (gd, gu, dg, ug, du, uu), outs, (wg, wu, rows, extra, sems) = (
            refs[:n],
            refs[n : n + 6],
            refs[n + 6 : n + 10],
            refs[n + 10 :],
        )
        fetch(early, ((dg.at[0], ug.at[0], wg), (du.at[0], uu.at[0], wu)), sems)
        me = lax.axis_index("tensor")
        gain = jnp.where(chosen(early), gd[...].astype(f32), gu[...].astype(f32))
        lane = lax.broadcasted_iota(jnp.int32, (1, 128), 1)
        start = 0
        for x in x_refs:
            size = x.shape[0]
            v = x[...].astype(f32)
            rows[pl.ds(start, size), :] = (v * gain).astype(bf16)
            total = jnp.sum(v * v, axis=1, keepdims=True)
            high = total.astype(bf16).astype(f32)
            extra[pl.ds(start, size), :] = jnp.where(lane < 64, high, total - high).astype(bf16)
            start += size
        for part, (w, source) in enumerate(((wg, dg), (wu, du))):
            pltpu.make_async_copy(source.at[0], w, sems.at[part]).wait()
            for k, out in enumerate(outs):
                at = pl.multiple_of(lax.rem(me + k, TENSOR) * count, count)
                out[:, pl.ds(part * width, width)] = jnp.dot(
                    rows[pl.ds(at, count), :], w[...], preferred_element_type=f32
                ).astype(bf16)
        for k, out in enumerate(outs):
            at = pl.multiple_of(lax.rem(me + k, TENSOR) * count, count)
            out[:, pl.ds(2 * width, 128)] = extra[pl.ds(at, count), :]

    return call(
        kernel,
        [((count, 2 * width + 128), bf16)] * TENSOR,
        [V] * (n + 2) + [A] * 4,
        [
            pltpu.VMEM((depth, width), bf16),
            pltpu.VMEM((depth, width), bf16),
            pltpu.VMEM((tokens, depth), bf16),
            pltpu.VMEM((tokens, 128), bf16),
            pltpu.SemaphoreType.DMA((2,)),
        ],
        flops=4 * tokens * depth * width,
        moved=4 * depth * width,
    )(*xs, *gains, *gates, *ups)


def hidden_of(parts, features):
    count, width = parts[0].shape[0], (parts[0].shape[1] - 128) // 2

    def kernel(a, b, c, d, out):
        refs = (a, b, c, d)
        tail = sum(r[:, pl.ds(2 * width, 128)].astype(f32) for r in refs)
        squares = tail[:, 0:1] + tail[:, 64:65]
        inverse = lax.rsqrt(squares / features + EPSILON)
        gate = sum(r[:, pl.ds(0, width)].astype(f32) for r in refs) * inverse
        up = sum(r[:, pl.ds(width, width)].astype(f32) for r in refs) * inverse
        out[...] = (gate / (1.0 + jnp.exp(-gate)) * up).astype(bf16)

    return call(kernel, [((count, width), bf16)], [V] * 4, moved=8 * count * width)(*parts)[0]


def down_part(hidden, projs, early):
    count, width = hidden[0].shape
    columns = projs[0].shape[2]
    half = count * TENSOR // 2

    def kernel(h0, h1, h2, h3, first, second, keep, send, w, rows, sems):
        fetch(early, ((first.at[0], second.at[0], w),), sems)
        me = lax.axis_index("tensor")
        for k, h in enumerate((h0, h1, h2, h3)):
            at = pl.multiple_of(lax.rem(me + TENSOR - k, TENSOR) * count, count)
            rows[pl.ds(at, count), :] = h[...]
        pltpu.make_async_copy(first.at[0], w, sems.at[0]).wait()
        send[...] = jnp.dot(
            rows[pl.ds(half, half), :], w[...], preferred_element_type=f32
        ).astype(bf16)
        keep[...] = jnp.dot(rows[pl.ds(0, half), :], w[...], preferred_element_type=f32)

    return call(
        kernel,
        [((half, columns), f32), ((half, columns), bf16)],
        [V] * 4 + [A] * 2,
        [
            pltpu.VMEM((width, columns), bf16),
            pltpu.VMEM((2 * half, width), bf16),
            pltpu.SemaphoreType.DMA((1,)),
        ],
        flops=4 * half * width * columns,
        moved=2 * width * columns,
    )(*hidden, *projs)


def add_and_split(keep, received):
    rows, columns = keep.shape
    chunk = rows // X

    def kernel(a, b, own, s1, s2, s3):
        own[...] = a[pl.ds(0, chunk), :] + b[pl.ds(0, chunk), :].astype(f32)
        for k, out in ((1, s1), (2, s2), (3, s3)):
            at = pl.ds((X - k) * chunk, chunk)
            out[...] = (a[at, :] + b[at, :].astype(f32)).astype(bf16)

    return call(
        kernel, [((chunk, columns), f32)] + [((chunk, columns), bf16)] * 3, [V] * 2, moved=6 * rows * columns
    )(keep, received)


def partial_sum(own, received, residual):
    def kernel(a, r1, r2, r3, x, out):
        zl = lax.rem(lax.axis_index("dp") // CORE, ZL)
        total = a[...] + r1[...].astype(f32) + r2[...].astype(f32) + r3[...].astype(f32)
        out[...] = (total + jnp.where(zl == 0, x[...].astype(f32), 0.0)).astype(bf16)

    return call(kernel, [(own.shape, bf16)], [V] * 5, moved=12 * own.size)(own, *received, residual)[0]


def pair_sum(a, b):
    def kernel(p, q, out):
        out[...] = (p[...].astype(f32) + q[...].astype(f32)).astype(bf16)

    return call(kernel, [(a.shape, bf16)], [V] * 2, moved=6 * a.size)(a, b)[0]


def local(
    down_input, up_input, down_gain, down_gate, down_up, down_proj, up_gain, up_gate, up_up, up_proj
):
    section = lax.axis_index("section")
    dp = lax.axis_index("dp")
    x_at, zl_at, core_at = dp // 4, dp // 2 % 2, dp % 2
    batches, tokens, width = down_input.shape
    per_data = tokens // 16
    features = width * TENSOR
    first = section < 2

    entry = jnp.where(first, down_input, up_input)
    entry = entry.reshape(batches, X, ZL, CORE, per_data, width).transpose(3, 1, 2, 0, 4, 5)
    entry = entry.reshape(CORE, X, ZL * batches * per_data, width)

    def chunk_of(core, j):
        return lax.dynamic_slice(
            entry, (core, (x_at + X - j) % X, 0, 0), (1, 1) + entry.shape[2:]
        ).reshape(entry.shape[2:])

    chunks = [chunk_of(core_at, j) for j in range(X)] + [chunk_of(1 - core_at, j) for j in range(X)]
    residual = chunks[0]
    xs = [jnp.concatenate(chunks, axis=0)]
    stored = []
    for tick in range(4):
        early = tick < 2
        parts = gate_up(xs, (down_gain, up_gain), (down_gate, up_gate), (down_up, up_up), early)
        parts = [parts[0]] + [
            along(parts[k], "tensor", ring(k, TENSOR)) for k in range(1, TENSOR)
        ]
        hidden = hidden_of(parts, features)
        hidden = [hidden] + [
            along(hidden, "tensor", ring(k, TENSOR)) for k in range(1, TENSOR)
        ]
        keep, send = down_part(hidden, (down_proj, up_proj), early)
        own, *sends = add_and_split(keep, along(send, "dp", CORE_PAIRS))
        received = [along(s, "dp", x_pairs(k + 1)) for k, s in enumerate(sends)]
        part = partial_sum(own, received, residual)
        if tick < 3:
            axes = ("dp", "section")
            near = along(part, axes, section_pairs(MOVES[tick], 0))
            far = along(part, axes, section_pairs(MOVES[tick], 2))
            residual = pair_sum(near, far)
            half = [residual] + [along(residual, "dp", x_pairs(k)) for k in range(1, X)]
            half = jnp.concatenate(half, axis=0)
            xs = [half, along(half, "dp", CORE_PAIRS)]
        count = batches * per_data
        mine = lax.dynamic_slice_in_dim(part, zl_at * count, count, 0)
        other = along(
            lax.dynamic_slice_in_dim(part, (1 - zl_at) * count, count, 0), "dp", ZL_PAIRS
        )
        stored.append((mine.astype(f32) + other.astype(f32)).astype(bf16))

    outer = (section == 0) | (section == 3)
    one = jnp.where(outer, stored[0], stored[1])
    two = jnp.where(outer, stored[3], stored[2])
    shape = (1, batches, per_data, width)
    return (
        jnp.where(first, one, two).reshape(shape),
        jnp.where(first, two, one).reshape(shape),
    )


def solution(mesh):
    placed = (
        P(None, None, "tensor"),
        P(None, None, "tensor"),
        P("section", "tensor"),
        P("section", "tensor", "dp"),
        P("section", "tensor", "dp"),
        P("section", "dp", "tensor"),
        P("section", "tensor"),
        P("section", "tensor", "dp"),
        P("section", "tensor", "dp"),
        P("section", "dp", "tensor"),
    )
    return jax.shard_map(
        local,
        mesh=mesh,
        in_specs=placed,
        out_specs=(P("section", None, "dp", "tensor"), P("section", None, "dp", "tensor")),
        check_vma=False,
    )
```

```python
import jax
import jax.numpy as jnp
from jax import lax
from jax.experimental import pallas as pl
from jax.experimental.pallas import tpu as pltpu
from jax.sharding import PartitionSpec as P

EPSILON = 1e-05
X, ZL, CORE, TENSOR = 4, 2, 2, 4
VMEM_LIMIT = 20 * 1024 * 1024
ENTER_LIMIT = 59 * 1024 * 1024
f32, bf16 = jnp.float32, jnp.bfloat16


def along(value, axis, pairs):
    return lax.ppermute(value, axis, pairs)


def ring(steps, count):
    return [(i, (i + steps) % count) for i in range(count)]


def x_pairs(steps):
    return [(i, (i + 4 * steps) % 16) for i in range(16)]


CORE_PAIRS = [(i, i ^ 1) for i in range(16)]
ZL_PAIRS = [(i, i ^ 2) for i in range(16)]


def section_pairs(moves, flip):
    return [(d * 4 + a, (d ^ flip) * 4 + b) for d in range(16) for a, b in moves]


OUTER = [(0, 1), (1, 0), (2, 3), (3, 2)]
MOVES = (OUTER, [(1, 2), (2, 1), (0, 3), (3, 0)], OUTER)


def call(kernel, outs, ins, scratch=(), flops=0, moved=0, grant=VMEM_LIMIT):
    return pl.pallas_call(
        kernel,
        out_shape=[jax.ShapeDtypeStruct(s, d) for s, d in outs],
        in_specs=ins,
        out_specs=[pl.BlockSpec(memory_space=pltpu.VMEM)] * len(outs),
        scratch_shapes=list(scratch),
        compiler_params=pltpu.CompilerParams(vmem_limit_bytes=grant),
        cost_estimate=pl.CostEstimate(flops=flops, bytes_accessed=moved, transcendentals=0),
    )


V = pl.BlockSpec(memory_space=pltpu.VMEM)
H = pl.BlockSpec(memory_space=pltpu.HBM)


def chosen(early):
    return (lax.axis_index("section") < 2) == early


def fetch(early, pairs, sems):
    down = chosen(early)

    @pl.when(down)
    def _():
        for n, (first, _, target) in enumerate(pairs):
            pltpu.make_async_copy(first, target, sems.at[n]).start()

    @pl.when(jnp.logical_not(down))
    def _():
        for n, (_, second, target) in enumerate(pairs):
            pltpu.make_async_copy(second, target, sems.at[n]).start()


def normalise(v, gain, start, rows, extra):
    lane = lax.broadcasted_iota(jnp.int32, (1, 128), 1)
    at = pl.ds(start, v.shape[0])
    rows[at, :] = (v * gain).astype(bf16)
    total = jnp.sum(v * v, axis=1, keepdims=True)
    high = total.astype(bf16).astype(f32)
    extra[at, :] = jnp.where(lane < 64, high, total - high).astype(bf16)


def share_products(rows, extra, weights, outs, wait=None):
    me = lax.axis_index("tensor")
    count, width = outs[0].shape[0], weights[0].shape[1]

    def share(k):
        return pl.ds(pl.multiple_of(lax.rem(me + k, TENSOR) * count, count), count)

    for k, out in enumerate(outs):
        out[:, pl.ds(2 * width, 128)] = extra[share(k), :]
    for part, w in enumerate(weights):
        if wait is not None:
            wait(part)
        for k, out in enumerate(outs):
            out[:, pl.ds(part * width, width)] = jnp.dot(
                rows[share(k), :], w[...], preferred_element_type=f32
            ).astype(bf16)


def enter(inputs, gains, gates, ups):
    batches, tokens, depth = inputs[0].shape
    width = gates[0].shape[2]
    total, per_data = batches * tokens, tokens // 16
    count, chunk = total // TENSOR, total // (CORE * X)

    def kernel(di, ui, gd, gu, dg, ug, du, uu, o0, o1, o2, o3, res, wg, wu, xin, xf, xr, rows, extra, sems):
        fetch(True, ((di, ui, xin), (dg.at[0], ug.at[0], wg), (du.at[0], uu.at[0], wu)), sems)
        gain = jnp.where(chosen(True), gd[...].astype(f32), gu[...].astype(f32))
        pltpu.make_async_copy(di, xin, sems.at[0]).wait()
        for batch in range(batches):
            xf[pl.ds(batch * tokens, tokens), :] = xin[batch].astype(f32)
        dp = lax.axis_index("dp")
        x_at, core_at = dp // (ZL * CORE), lax.rem(dp, CORE)
        for c in range(CORE):
            core = core_at if c == 0 else 1 - core_at
            for j in range(X):
                group = lax.rem(x_at + X - j, X) * (ZL * CORE) + core
                for zl in range(ZL):
                    for batch in range(batches):
                        source = pl.multiple_of(batch * tokens + (group + zl * CORE) * per_data, per_data)
                        target = (((c * X + j) * ZL + zl) * batches + batch) * per_data
                        xr[pl.ds(target, per_data), :] = xf[pl.ds(source, per_data), :]
        normalise(xr[...], gain, 0, rows, extra)
        res[...] = xr[pl.ds(0, chunk), :].astype(bf16)

        def wait(part):
            pltpu.make_async_copy((dg, du)[part].at[0], (wg, wu)[part], sems.at[1 + part]).wait()

        share_products(rows, extra, (wg, wu), (o0, o1, o2, o3), wait)

    return call(
        kernel,
        [((count, 2 * width + 128), bf16)] * TENSOR + [((chunk, depth), bf16)],
        [H] * 2 + [V] * 2 + [H] * 4,
        [
            pltpu.VMEM((depth, width), bf16),
            pltpu.VMEM((depth, width), bf16),
            pltpu.VMEM((batches, tokens, depth), bf16),
            pltpu.VMEM((total, depth), f32),
            pltpu.VMEM((total, depth), f32),
            pltpu.VMEM((total, depth), bf16),
            pltpu.VMEM((total, 128), bf16),
            pltpu.SemaphoreType.DMA((3,)),
        ],
        flops=4 * total * depth * width,
        moved=6 * depth * width,
        grant=ENTER_LIMIT,
    )(*inputs, *gains, *gates, *ups)


def gate_up(xs, gains, gates, ups, early):
    tokens = sum(x.shape[0] for x in xs)
    depth, width = gates[0].shape[1:]
    count = tokens // TENSOR

    def kernel(xa, xb, gd, gu, dg, ug, du, uu, o0, o1, o2, o3, rows, extra):
        down = chosen(early)
        gain = jnp.where(down, gd[...].astype(f32), gu[...].astype(f32))
        normalise(xa[...].astype(f32), gain, 0, rows, extra)
        normalise(xb[...].astype(f32), gain, xa.shape[0], rows, extra)

        @pl.when(down)
        def _():
            share_products(rows, extra, (dg.at[0], du.at[0]), (o0, o1, o2, o3))

        @pl.when(jnp.logical_not(down))
        def _():
            share_products(rows, extra, (ug.at[0], uu.at[0]), (o0, o1, o2, o3))

    return call(
        kernel,
        [((count, 2 * width + 128), bf16)] * TENSOR,
        [V] * 8,
        [pltpu.VMEM((tokens, depth), bf16), pltpu.VMEM((tokens, 128), bf16)],
        flops=4 * tokens * depth * width,
        moved=4 * depth * width,
    )(*xs, *gains, *gates, *ups)


def hidden_of(parts, features):
    count, width = parts[0].shape[0], (parts[0].shape[1] - 128) // 2

    def kernel(a, b, c, d, out):
        refs = (a, b, c, d)
        tail = sum(r[:, pl.ds(2 * width, 128)].astype(f32) for r in refs)
        squares = tail[:, 0:1] + tail[:, 64:65]
        inverse = lax.rsqrt(squares / features + EPSILON)
        gate = sum(r[:, pl.ds(0, width)].astype(f32) for r in refs) * inverse
        up = sum(r[:, pl.ds(width, width)].astype(f32) for r in refs) * inverse
        out[...] = (gate / (1.0 + jnp.exp(-gate)) * up).astype(bf16)

    return call(kernel, [((count, width), bf16)], [V] * 4, moved=8 * count * width)(*parts)[0]


def down_part(hidden, projs, early):
    count, width = hidden[0].shape
    columns = projs[0].shape[2]
    half = count * TENSOR // 2

    def kernel(h0, h1, h2, h3, first, second, keep, send, rows):
        me = lax.axis_index("tensor")
        for k, h in enumerate((h0, h1, h2, h3)):
            at = pl.multiple_of(lax.rem(me + TENSOR - k, TENSOR) * count, count)
            rows[pl.ds(at, count), :] = h[...]

        def products(w):
            send[...] = jnp.dot(
                rows[pl.ds(half, half), :], w[0], preferred_element_type=f32
            ).astype(bf16)
            keep[...] = jnp.dot(rows[pl.ds(0, half), :], w[0], preferred_element_type=f32)

        down = chosen(early)

        @pl.when(down)
        def _():
            products(first)

        @pl.when(jnp.logical_not(down))
        def _():
            products(second)

    return call(
        kernel,
        [((half, columns), f32), ((half, columns), bf16)],
        [V] * 6,
        [pltpu.VMEM((2 * half, width), bf16)],
        flops=4 * half * width * columns,
        moved=2 * width * columns,
    )(*hidden, *projs)


def add_and_split(keep, received):
    rows, columns = keep.shape
    chunk = rows // X

    def kernel(a, b, own, s1, s2, s3):
        own[...] = a[pl.ds(0, chunk), :] + b[pl.ds(0, chunk), :].astype(f32)
        for k, out in ((1, s1), (2, s2), (3, s3)):
            at = pl.ds((X - k) * chunk, chunk)
            out[...] = (a[at, :] + b[at, :].astype(f32)).astype(bf16)

    return call(
        kernel, [((chunk, columns), f32)] + [((chunk, columns), bf16)] * 3, [V] * 2, moved=6 * rows * columns
    )(keep, received)


def partial_sum(own, received, residual, stored=None):
    def total(a, r1, r2, r3, x):
        zl = lax.rem(lax.axis_index("dp") // CORE, ZL)
        value = a[...] + r1[...].astype(f32) + r2[...].astype(f32) + r3[...].astype(f32)
        return zl, (value + jnp.where(zl == 0, x[...].astype(f32), 0.0)).astype(bf16)

    if stored is None:

        def kernel(a, r1, r2, r3, x, out):
            out[...] = total(a, r1, r2, r3, x)[1]

        return call(kernel, [(own.shape, bf16)], [V] * 5, moved=12 * own.size)(own, *received, residual)[0]

    count = own.shape[0] // ZL

    def last(a, r1, r2, r3, x, p0, p1, p2, keep, send, scratch):
        zl, p3 = total(a, r1, r2, r3, x)
        section = lax.axis_index("section")
        outer = jnp.logical_or(section == 0, section == 3)
        scratch[0] = jnp.where(outer, p0[...], p1[...])
        scratch[1] = jnp.where(outer, p3, p2[...])
        mine = pl.ds(pl.multiple_of(zl * count, count), count)
        other = pl.ds(pl.multiple_of((1 - zl) * count, count), count)
        for n in range(2):
            keep[pl.ds(n * count, count), :] = scratch[n, mine, :]
            send[pl.ds(n * count, count), :] = scratch[n, other, :]

    return call(
        last,
        [(own.shape, bf16)] * 2,
        [V] * 8,
        [pltpu.VMEM((2,) + own.shape, bf16)],
        moved=20 * own.size,
    )(own, *received, residual, *stored)


def leave(keep, received, batches):
    count, columns = keep.shape[0] // 2, keep.shape[1]
    size = count // batches

    def kernel(a, b, down, up):
        first = lax.axis_index("section") < 2
        value = a[...].astype(f32) + b[...].astype(f32)
        one, two = value[:count], value[count:]
        for out, rows in ((down, jnp.where(first, one, two)), (up, jnp.where(first, two, one))):
            for batch in range(batches):
                out[0, batch] = rows[batch * size : (batch + 1) * size].astype(bf16)

    return call(
        kernel, [((1, batches, size, columns), bf16)] * 2, [V] * 2, moved=8 * keep.size
    )(keep, received)


def pair_sum(a, b):
    def kernel(p, q, out):
        out[...] = (p[...].astype(f32) + q[...].astype(f32)).astype(bf16)

    return call(kernel, [(a.shape, bf16)], [V] * 2, moved=6 * a.size)(a, b)[0]


def local(
    down_input, up_input, down_gain, down_gate, down_up, down_proj, up_gain, up_gate, up_up, up_proj
):
    features = down_input.shape[2] * TENSOR
    gains = (down_gain, up_gain)
    gates, ups, projs = (down_gate, up_gate), (down_up, up_up), (down_proj, up_proj)
    stored = []
    for tick in range(4):
        early = tick < 2
        if tick == 0:
            *parts, residual = enter((down_input, up_input), gains, gates, ups)
        else:
            parts = gate_up(xs, gains, gates, ups, early)
        parts = [parts[0]] + [along(parts[k], "tensor", ring(k, TENSOR)) for k in range(1, TENSOR)]
        hidden = hidden_of(parts, features)
        hidden = [hidden] + [along(hidden, "tensor", ring(k, TENSOR)) for k in range(1, TENSOR)]
        keep, send = down_part(hidden, projs, early)
        own, *sends = add_and_split(keep, along(send, "dp", CORE_PAIRS))
        received = [along(s, "dp", x_pairs(k + 1)) for k, s in enumerate(sends)]
        if tick == 3:
            keep, send = partial_sum(own, received, residual, stored)
            return leave(keep, along(send, "dp", ZL_PAIRS), down_input.shape[0])
        part = partial_sum(own, received, residual)
        stored.append(part)
        near = along(part, ("dp", "section"), section_pairs(MOVES[tick], 0))
        far = along(part, ("dp", "section"), section_pairs(MOVES[tick], 2))
        residual = pair_sum(near, far)
        half = [residual] + [along(residual, "dp", x_pairs(k)) for k in range(1, X)]
        half = jnp.concatenate(half, axis=0)
        xs = [half, along(half, "dp", CORE_PAIRS)]


def solution(mesh):
    placed = (
        P(None, None, "tensor"),
        P(None, None, "tensor"),
        P("section", "tensor"),
        P("section", "tensor", "dp"),
        P("section", "tensor", "dp"),
        P("section", "dp", "tensor"),
        P("section", "tensor"),
        P("section", "tensor", "dp"),
        P("section", "tensor", "dp"),
        P("section", "dp", "tensor"),
    )
    return jax.shard_map(
        local,
        mesh=mesh,
        in_specs=placed,
        out_specs=(P("section", None, "dp", "tensor"), P("section", None, "dp", "tensor")),
        check_vma=False,
    )
```

```python
import jax
import jax.numpy as jnp
from jax import lax
from jax.experimental import pallas as pl
from jax.experimental.pallas import tpu as pltpu
from jax.sharding import PartitionSpec as P

EPSILON = 1e-05
X, ZL, CORE, TENSOR = 4, 2, 2, 4
VMEM_LIMIT = 20 * 1024 * 1024
ENTER_LIMIT = 59 * 1024 * 1024
f32, bf16 = jnp.float32, jnp.bfloat16


def along(value, axis, pairs):
    return lax.ppermute(value, axis, pairs)


def ring(steps, count):
    return [(i, (i + steps) % count) for i in range(count)]


def x_pairs(steps):
    return [(i, (i + 4 * steps) % 16) for i in range(16)]


CORE_PAIRS = [(i, i ^ 1) for i in range(16)]
ZL_PAIRS = [(i, i ^ 2) for i in range(16)]


def section_pairs(moves, flip):
    return [(d * 4 + a, (d ^ flip) * 4 + b) for d in range(16) for a, b in moves]


OUTER = [(0, 1), (1, 0), (2, 3), (3, 2)]
MOVES = (OUTER, [(1, 2), (2, 1), (0, 3), (3, 0)], OUTER)


def call(kernel, outs, ins, scratch=(), flops=0, moved=0, grant=VMEM_LIMIT):
    return pl.pallas_call(
        kernel,
        out_shape=[jax.ShapeDtypeStruct(s, d) for s, d in outs],
        in_specs=ins,
        out_specs=[pl.BlockSpec(memory_space=pltpu.VMEM)] * len(outs),
        scratch_shapes=list(scratch),
        compiler_params=pltpu.CompilerParams(vmem_limit_bytes=grant),
        cost_estimate=pl.CostEstimate(flops=flops, bytes_accessed=moved, transcendentals=0),
    )


V = pl.BlockSpec(memory_space=pltpu.VMEM)
H = pl.BlockSpec(memory_space=pltpu.HBM)


def chosen(early):
    return (lax.axis_index("section") < 2) == early


def fetch(early, pairs, sems):
    down = chosen(early)

    @pl.when(down)
    def _():
        for n, (first, _, target) in enumerate(pairs):
            pltpu.make_async_copy(first, target, sems.at[n]).start()

    @pl.when(jnp.logical_not(down))
    def _():
        for n, (_, second, target) in enumerate(pairs):
            pltpu.make_async_copy(second, target, sems.at[n]).start()


def normalise(v, gain, first, rows, extra):
    me = lax.axis_index("tensor")
    count = rows.shape[0] // TENSOR
    lane = lax.broadcasted_iota(jnp.int32, (1, 128), 1)
    for n in range(v.shape[0] // count):
        part = v[n * count : (n + 1) * count]
        at = pl.ds(pl.multiple_of(lax.rem(first + n + TENSOR - me, TENSOR) * count, count), count)
        rows[at, :] = (part * gain).astype(bf16)
        total = jnp.sum(part * part, axis=1, keepdims=True)
        high = total.astype(bf16).astype(f32)
        extra[at, :] = jnp.where(lane < 64, high, total - high).astype(bf16)


def share_products(rows, extra, weights, outs, wait=None):
    count, width = outs[0].shape[0], weights[0].shape[1]
    for k, out in enumerate(outs):
        out[:, pl.ds(2 * width, 128)] = extra[pl.ds(k * count, count), :]
    for part, w in enumerate(weights):
        if wait is not None:
            wait(part)
        product = jnp.dot(rows[...], w[...], preferred_element_type=f32).astype(bf16)
        for k, out in enumerate(outs):
            out[:, pl.ds(part * width, width)] = product[k * count : (k + 1) * count]


def enter(inputs, gains, gates, ups):
    batches, tokens, depth = inputs[0].shape
    width = gates[0].shape[2]
    total, per_data = batches * tokens, tokens // 16
    count, chunk = total // TENSOR, total // (CORE * X)

    def kernel(di, ui, gd, gu, dg, ug, du, uu, o0, o1, o2, o3, res, wg, wu, xin, xf, xr, rows, extra, sems):
        fetch(True, ((di, ui, xin), (dg.at[0], ug.at[0], wg), (du.at[0], uu.at[0], wu)), sems)
        gain = jnp.where(chosen(True), gd[...].astype(f32), gu[...].astype(f32))
        pltpu.make_async_copy(di, xin, sems.at[0]).wait()
        for batch in range(batches):
            xf[pl.ds(batch * tokens, tokens), :] = xin[batch].astype(f32)
        dp = lax.axis_index("dp")
        x_at, core_at = dp // (ZL * CORE), lax.rem(dp, CORE)
        for c in range(CORE):
            core = core_at if c == 0 else 1 - core_at
            for j in range(X):
                group = lax.rem(x_at + X - j, X) * (ZL * CORE) + core
                for zl in range(ZL):
                    for batch in range(batches):
                        source = pl.multiple_of(batch * tokens + (group + zl * CORE) * per_data, per_data)
                        target = (((c * X + j) * ZL + zl) * batches + batch) * per_data
                        xr[pl.ds(target, per_data), :] = xf[pl.ds(source, per_data), :]
        normalise(xr[...], gain, 0, rows, extra)
        res[...] = xr[pl.ds(0, chunk), :].astype(bf16)

        def wait(part):
            pltpu.make_async_copy((dg, du)[part].at[0], (wg, wu)[part], sems.at[1 + part]).wait()

        share_products(rows, extra, (wg, wu), (o0, o1, o2, o3), wait)

    return call(
        kernel,
        [((count, 2 * width + 128), bf16)] * TENSOR + [((chunk, depth), bf16)],
        [H] * 2 + [V] * 2 + [H] * 4,
        [
            pltpu.VMEM((depth, width), bf16),
            pltpu.VMEM((depth, width), bf16),
            pltpu.VMEM((batches, tokens, depth), bf16),
            pltpu.VMEM((total, depth), f32),
            pltpu.VMEM((total, depth), f32),
            pltpu.VMEM((total, depth), bf16),
            pltpu.VMEM((total, 128), bf16),
            pltpu.SemaphoreType.DMA((3,)),
        ],
        flops=4 * total * depth * width,
        moved=6 * depth * width,
        grant=ENTER_LIMIT,
    )(*inputs, *gains, *gates, *ups)


def gate_up(xs, gains, gates, ups, early):
    tokens = sum(x.shape[0] for x in xs)
    depth, width = gates[0].shape[1:]
    count = tokens // TENSOR

    def kernel(xa, xb, gd, gu, dg, ug, du, uu, o0, o1, o2, o3, rows, extra):
        down = chosen(early)
        gain = jnp.where(down, gd[...].astype(f32), gu[...].astype(f32))
        normalise(xa[...].astype(f32), gain, 0, rows, extra)
        normalise(xb[...].astype(f32), gain, TENSOR // 2, rows, extra)

        @pl.when(down)
        def _():
            share_products(rows, extra, (dg.at[0], du.at[0]), (o0, o1, o2, o3))

        @pl.when(jnp.logical_not(down))
        def _():
            share_products(rows, extra, (ug.at[0], uu.at[0]), (o0, o1, o2, o3))

    return call(
        kernel,
        [((count, 2 * width + 128), bf16)] * TENSOR,
        [V] * 8,
        [pltpu.VMEM((tokens, depth), bf16), pltpu.VMEM((tokens, 128), bf16)],
        flops=4 * tokens * depth * width,
        moved=4 * depth * width,
    )(*xs, *gains, *gates, *ups)


def hidden_of(parts, features):
    count, width = parts[0].shape[0], (parts[0].shape[1] - 128) // 2

    def kernel(a, b, c, d, *outs):
        refs = (a, b, c, d)
        tail = sum(r[:, pl.ds(2 * width, 128)].astype(f32) for r in refs)
        squares = tail[:, 0:1] + tail[:, 64:65]
        inverse = lax.rsqrt(squares / features + EPSILON)
        gate = sum(r[:, pl.ds(0, width)].astype(f32) for r in refs) * inverse
        up = sum(r[:, pl.ds(width, width)].astype(f32) for r in refs) * inverse
        value = (gate / (1.0 + jnp.exp(-gate)) * up).astype(bf16)
        for out in outs:
            out[...] = value

    return call(kernel, [((count, width), bf16)] * TENSOR, [V] * 4, moved=8 * count * width)(*parts)


def down_part(hidden, projs, early, side, dtype):
    count, width = hidden[0].shape
    columns = projs[0].shape[2]
    half = count * TENSOR // 2

    def kernel(h0, h1, h2, h3, first, second, out, rows):
        me = lax.axis_index("tensor")
        for k, h in enumerate((h0, h1, h2, h3)):
            at = pl.multiple_of(lax.rem(me + TENSOR - k, TENSOR) * count, count)
            rows[pl.ds(at, count), :] = h[...]
        down = chosen(early)

        @pl.when(down)
        def _():
            out[...] = jnp.dot(
                rows[pl.ds(side * half, half), :], first[0], preferred_element_type=f32
            ).astype(dtype)

        @pl.when(jnp.logical_not(down))
        def _():
            out[...] = jnp.dot(
                rows[pl.ds(side * half, half), :], second[0], preferred_element_type=f32
            ).astype(dtype)

    return call(
        kernel,
        [((half, columns), dtype)],
        [V] * 6,
        [pltpu.VMEM((2 * half, width), bf16)],
        flops=2 * half * width * columns,
        moved=2 * width * columns,
    )(*hidden, *projs)[0]


def add_and_split(keep, received):
    rows, columns = keep.shape
    chunk = rows // X

    def kernel(a, b, own, s1, s2, s3):
        own[...] = a[pl.ds(0, chunk), :] + b[pl.ds(0, chunk), :].astype(f32)
        for k, out in ((1, s1), (2, s2), (3, s3)):
            at = pl.ds((X - k) * chunk, chunk)
            out[...] = (a[at, :] + b[at, :].astype(f32)).astype(bf16)

    return call(
        kernel, [((chunk, columns), f32)] + [((chunk, columns), bf16)] * 3, [V] * 2, moved=6 * rows * columns
    )(keep, received)


def partial_sum(own, received, residual, stored=None):
    def total(a, r1, r2, r3, x):
        zl = lax.rem(lax.axis_index("dp") // CORE, ZL)
        value = a[...] + r1[...].astype(f32) + r2[...].astype(f32) + r3[...].astype(f32)
        return zl, (value + jnp.where(zl == 0, x[...].astype(f32), 0.0)).astype(bf16)

    if stored is None:

        def kernel(a, r1, r2, r3, x, out):
            out[...] = total(a, r1, r2, r3, x)[1]

        return call(kernel, [(own.shape, bf16)], [V] * 5, moved=12 * own.size)(own, *received, residual)[0]

    count = own.shape[0] // ZL

    def last(a, r1, r2, r3, x, p0, p1, p2, keep, send, scratch):
        zl, p3 = total(a, r1, r2, r3, x)
        section = lax.axis_index("section")
        outer = jnp.logical_or(section == 0, section == 3)
        scratch[0] = jnp.where(outer, p0[...], p1[...])
        scratch[1] = jnp.where(outer, p3, p2[...])
        mine = pl.ds(pl.multiple_of(zl * count, count), count)
        other = pl.ds(pl.multiple_of((1 - zl) * count, count), count)
        for n in range(2):
            keep[pl.ds(n * count, count), :] = scratch[n, mine, :]
            send[pl.ds(n * count, count), :] = scratch[n, other, :]

    return call(
        last,
        [(own.shape, bf16)] * 2,
        [V] * 8,
        [pltpu.VMEM((2,) + own.shape, bf16)],
        moved=20 * own.size,
    )(own, *received, residual, *stored)


def leave(keep, received, batches):
    count, columns = keep.shape[0] // 2, keep.shape[1]
    size = count // batches

    def kernel(a, b, down, up):
        first = lax.axis_index("section") < 2
        value = a[...].astype(f32) + b[...].astype(f32)
        one, two = value[:count], value[count:]
        for out, rows in ((down, jnp.where(first, one, two)), (up, jnp.where(first, two, one))):
            for batch in range(batches):
                out[0, batch] = rows[batch * size : (batch + 1) * size].astype(bf16)

    return call(
        kernel, [((1, batches, size, columns), bf16)] * 2, [V] * 2, moved=8 * keep.size
    )(keep, received)


def pair_sum(a, b):
    def kernel(p, q, *outs):
        value = (p[...].astype(f32) + q[...].astype(f32)).astype(bf16)
        for out in outs:
            out[...] = value

    return call(kernel, [(a.shape, bf16)] * X, [V] * 2, moved=6 * a.size)(a, b)


def local(
    down_input, up_input, down_gain, down_gate, down_up, down_proj, up_gain, up_gate, up_up, up_proj
):
    features = down_input.shape[2] * TENSOR
    gains = (down_gain, up_gain)
    gates, ups, projs = (down_gate, up_gate), (down_up, up_up), (down_proj, up_proj)
    stored = []
    for tick in range(4):
        early = tick < 2
        if tick == 0:
            *parts, residual = enter((down_input, up_input), gains, gates, ups)
        else:
            parts = gate_up(xs, gains, gates, ups, early)
        parts = [parts[0]] + [along(parts[k], "tensor", ring(k, TENSOR)) for k in range(1, TENSOR)]
        hidden = hidden_of(parts, features)
        hidden = [hidden[0]] + [along(hidden[k], "tensor", ring(k, TENSOR)) for k in range(1, TENSOR)]
        other = along(down_part(hidden, projs, early, 1, bf16), "dp", CORE_PAIRS)
        own, *sends = add_and_split(down_part(hidden, projs, early, 0, f32), other)
        received = [along(s, "dp", x_pairs(k + 1)) for k, s in enumerate(sends)]
        if tick == 3:
            keep, send = partial_sum(own, received, residual, stored)
            return leave(keep, along(send, "dp", ZL_PAIRS), down_input.shape[0])
        part = partial_sum(own, received, residual)
        stored.append(part)
        near = along(part, ("dp", "section"), section_pairs(MOVES[tick], 0))
        far = along(part, ("dp", "section"), section_pairs(MOVES[tick], 2))
        residual, *copies = pair_sum(near, far)
        half = [residual] + [along(c, "dp", x_pairs(k + 1)) for k, c in enumerate(copies)]
        half = jnp.concatenate(half, axis=0)
        xs = [half, along(half, "dp", CORE_PAIRS)]


def solution(mesh):
    placed = (
        P(None, None, "tensor"),
        P(None, None, "tensor"),
        P("section", "tensor"),
        P("section", "tensor", "dp"),
        P("section", "tensor", "dp"),
        P("section", "dp", "tensor"),
        P("section", "tensor"),
        P("section", "tensor", "dp"),
        P("section", "tensor", "dp"),
        P("section", "dp", "tensor"),
    )
    return jax.shard_map(
        local,
        mesh=mesh,
        in_specs=placed,
        out_specs=(P("section", None, "dp", "tensor"), P("section", None, "dp", "tensor")),
        check_vma=False,
    )
```

```python
import jax
import jax.numpy as jnp
from jax import lax
from jax.experimental import pallas as pl
from jax.experimental.pallas import tpu as pltpu
from jax.sharding import PartitionSpec as P

EPSILON = 1e-05
X, ZL, CORE, TENSOR = 4, 2, 2, 4
VMEM_LIMIT = 20 * 1024 * 1024
ENTER_LIMIT = 59 * 1024 * 1024
f32, bf16 = jnp.float32, jnp.bfloat16


def along(value, axis, pairs):
    return lax.ppermute(value, axis, pairs)


def tensor_pairs(k):
    return [(i, i ^ k) for i in range(TENSOR)]


def exchanged(shares):
    return [shares[0]] + [
        along(share, "tensor", tensor_pairs(k)) for k, share in zip(TENSOR_ORDER, shares[1:])
    ]


def x_pairs(steps):
    return [(i, (i + 4 * steps) % 16) for i in range(16)]


TENSOR_ORDER = (1, 3, 2)
CORE_PAIRS = [(i, i ^ 1) for i in range(16)]
ZL_PAIRS = [(i, i ^ 2) for i in range(16)]


def section_pairs(moves, flip):
    return [(d * 4 + a, (d ^ flip) * 4 + b) for d in range(16) for a, b in moves]


OUTER = [(0, 1), (1, 0), (2, 3), (3, 2)]
MOVES = (OUTER, [(1, 2), (2, 1), (0, 3), (3, 0)], OUTER)


def call(kernel, outs, ins, scratch=(), flops=0, moved=0, grant=VMEM_LIMIT):
    return pl.pallas_call(
        kernel,
        out_shape=[jax.ShapeDtypeStruct(s, d) for s, d in outs],
        in_specs=ins,
        out_specs=[pl.BlockSpec(memory_space=pltpu.VMEM)] * len(outs),
        scratch_shapes=list(scratch),
        compiler_params=pltpu.CompilerParams(vmem_limit_bytes=grant),
        cost_estimate=pl.CostEstimate(flops=flops, bytes_accessed=moved, transcendentals=0),
    )


V = pl.BlockSpec(memory_space=pltpu.VMEM)
H = pl.BlockSpec(memory_space=pltpu.HBM)


def chosen(early):
    return (lax.axis_index("section") < 2) == early


def fetch(early, pairs, sems):
    down = chosen(early)

    @pl.when(down)
    def _():
        for n, (first, _, target) in enumerate(pairs):
            pltpu.make_async_copy(first, target, sems.at[n]).start()

    @pl.when(jnp.logical_not(down))
    def _():
        for n, (_, second, target) in enumerate(pairs):
            pltpu.make_async_copy(second, target, sems.at[n]).start()


def normalise(v, gain, first, rows, extra):
    me = lax.axis_index("tensor")
    count = rows.shape[0] // TENSOR
    lane = lax.broadcasted_iota(jnp.int32, (1, 128), 1)
    for n in range(v.shape[0] // count):
        part = v[n * count : (n + 1) * count]
        at = pl.ds(pl.multiple_of(lax.bitwise_xor(first + n, me) * count, count), count)
        rows[at, :] = (part * gain).astype(bf16)
        total = jnp.sum(part * part, axis=1, keepdims=True)
        high = total.astype(bf16).astype(f32)
        extra[at, :] = jnp.where(lane < 64, high, total - high).astype(bf16)


def share_products(rows, extra, weights, outs, wait=None):
    count, width = outs[0].shape[0], weights[0].shape[1]
    outs = tuple(zip((0,) + TENSOR_ORDER, outs))
    for k, out in outs:
        out[:, pl.ds(2 * width, 128)] = extra[pl.ds(k * count, count), :]
    for part, w in enumerate(weights):
        if wait is not None:
            wait(part)
        product = jnp.dot(rows[...], w[...], preferred_element_type=f32).astype(bf16)
        for k, out in outs:
            out[:, pl.ds(part * width, width)] = product[k * count : (k + 1) * count]


def enter(inputs, gains, gates, ups):
    batches, tokens, depth = inputs[0].shape
    width = gates[0].shape[2]
    total, per_data = batches * tokens, tokens // 16
    count, chunk = total // TENSOR, total // (CORE * X)

    def kernel(di, ui, gd, gu, dg, ug, du, uu, o0, o1, o2, o3, res, wg, wu, xin, xf, xr, rows, extra, sems):
        fetch(True, ((di, ui, xin), (dg.at[0], ug.at[0], wg), (du.at[0], uu.at[0], wu)), sems)
        gain = jnp.where(chosen(True), gd[...].astype(f32), gu[...].astype(f32))
        pltpu.make_async_copy(di, xin, sems.at[0]).wait()
        for batch in range(batches):
            xf[pl.ds(batch * tokens, tokens), :] = xin[batch].astype(f32)
        dp = lax.axis_index("dp")
        x_at, core_at = dp // (ZL * CORE), lax.rem(dp, CORE)
        for c in range(CORE):
            core = core_at if c == 0 else 1 - core_at
            for j in range(X):
                group = lax.rem(x_at + X - j, X) * (ZL * CORE) + core
                for zl in range(ZL):
                    for batch in range(batches):
                        source = pl.multiple_of(batch * tokens + (group + zl * CORE) * per_data, per_data)
                        target = (((c * X + j) * ZL + zl) * batches + batch) * per_data
                        xr[pl.ds(target, per_data), :] = xf[pl.ds(source, per_data), :]
        normalise(xr[...], gain, 0, rows, extra)
        res[...] = xr[pl.ds(0, chunk), :].astype(bf16)

        def wait(part):
            pltpu.make_async_copy((dg, du)[part].at[0], (wg, wu)[part], sems.at[1 + part]).wait()

        share_products(rows, extra, (wg, wu), (o0, o1, o2, o3), wait)

    return call(
        kernel,
        [((count, 2 * width + 128), bf16)] * TENSOR + [((chunk, depth), bf16)],
        [H] * 2 + [V] * 2 + [H] * 4,
        [
            pltpu.VMEM((depth, width), bf16),
            pltpu.VMEM((depth, width), bf16),
            pltpu.VMEM((batches, tokens, depth), bf16),
            pltpu.VMEM((total, depth), f32),
            pltpu.VMEM((total, depth), f32),
            pltpu.VMEM((total, depth), bf16),
            pltpu.VMEM((total, 128), bf16),
            pltpu.SemaphoreType.DMA((3,)),
        ],
        flops=4 * total * depth * width,
        moved=6 * depth * width,
        grant=ENTER_LIMIT,
    )(*inputs, *gains, *gates, *ups)


def gate_up(xs, gains, gates, ups, early):
    tokens = sum(x.shape[0] for x in xs)
    depth, width = gates[0].shape[1:]
    count = tokens // TENSOR

    def kernel(xa, xb, gd, gu, dg, ug, du, uu, o0, o1, o2, o3, rows, extra):
        down = chosen(early)
        gain = jnp.where(down, gd[...].astype(f32), gu[...].astype(f32))
        normalise(xa[...].astype(f32), gain, 0, rows, extra)
        normalise(xb[...].astype(f32), gain, TENSOR // 2, rows, extra)

        @pl.when(down)
        def _():
            share_products(rows, extra, (dg.at[0], du.at[0]), (o0, o1, o2, o3))

        @pl.when(jnp.logical_not(down))
        def _():
            share_products(rows, extra, (ug.at[0], uu.at[0]), (o0, o1, o2, o3))

    return call(
        kernel,
        [((count, 2 * width + 128), bf16)] * TENSOR,
        [V] * 8,
        [pltpu.VMEM((tokens, depth), bf16), pltpu.VMEM((tokens, 128), bf16)],
        flops=4 * tokens * depth * width,
        moved=4 * depth * width,
    )(*xs, *gains, *gates, *ups)


def hidden_of(parts, features):
    count, width = parts[0].shape[0], (parts[0].shape[1] - 128) // 2

    def kernel(a, b, c, d, *outs):
        refs = (a, b, c, d)
        tail = sum(r[:, pl.ds(2 * width, 128)].astype(f32) for r in refs)
        squares = tail[:, 0:1] + tail[:, 64:65]
        inverse = lax.rsqrt(squares / features + EPSILON)
        gate = sum(r[:, pl.ds(0, width)].astype(f32) for r in refs) * inverse
        up = sum(r[:, pl.ds(width, width)].astype(f32) for r in refs) * inverse
        value = (gate / (1.0 + jnp.exp(-gate)) * up).astype(bf16)
        for out in outs:
            out[...] = value

    return call(kernel, [((count, width), bf16)] * TENSOR, [V] * 4, moved=8 * count * width)(*parts)


def down_part(hidden, projs, early, side, dtype):
    count, width = hidden[0].shape
    columns = projs[0].shape[2]
    half = count * TENSOR // 2

    def kernel(h0, h1, h2, h3, first, second, out, rows):
        me = lax.axis_index("tensor")
        for k, h in zip((0,) + TENSOR_ORDER, (h0, h1, h2, h3)):
            at = pl.multiple_of(lax.bitwise_xor(me, k) * count, count)
            rows[pl.ds(at, count), :] = h[...]
        down = chosen(early)

        @pl.when(down)
        def _():
            out[...] = jnp.dot(
                rows[pl.ds(side * half, half), :], first[0], preferred_element_type=f32
            ).astype(dtype)

        @pl.when(jnp.logical_not(down))
        def _():
            out[...] = jnp.dot(
                rows[pl.ds(side * half, half), :], second[0], preferred_element_type=f32
            ).astype(dtype)

    return call(
        kernel,
        [((half, columns), dtype)],
        [V] * 6,
        [pltpu.VMEM((2 * half, width), bf16)],
        flops=2 * half * width * columns,
        moved=2 * width * columns,
    )(*hidden, *projs)[0]


def add_and_split(keep, received):
    rows, columns = keep.shape
    chunk = rows // X

    def kernel(a, b, own, s1, s2, s3):
        own[...] = a[pl.ds(0, chunk), :] + b[pl.ds(0, chunk), :].astype(f32)
        for k, out in ((1, s1), (2, s2), (3, s3)):
            at = pl.ds((X - k) * chunk, chunk)
            out[...] = (a[at, :] + b[at, :].astype(f32)).astype(bf16)

    return call(
        kernel, [((chunk, columns), f32)] + [((chunk, columns), bf16)] * 3, [V] * 2, moved=6 * rows * columns
    )(keep, received)


def partial_sum(own, received, residual, stored=None):
    def total(a, r1, r2, r3, x):
        zl = lax.rem(lax.axis_index("dp") // CORE, ZL)
        value = a[...] + r1[...].astype(f32) + r2[...].astype(f32) + r3[...].astype(f32)
        return zl, (value + jnp.where(zl == 0, x[...].astype(f32), 0.0)).astype(bf16)

    if stored is None:

        def kernel(a, r1, r2, r3, x, near, far, kept):
            value = total(a, r1, r2, r3, x)[1]
            near[...] = value
            far[...] = value
            kept[...] = value

        return call(kernel, [(own.shape, bf16)] * 3, [V] * 5, moved=12 * own.size)(own, *received, residual)

    count = own.shape[0] // ZL

    def last(a, r1, r2, r3, x, p0, p1, p2, keep, send, scratch):
        zl, p3 = total(a, r1, r2, r3, x)
        section = lax.axis_index("section")
        outer = jnp.logical_or(section == 0, section == 3)
        scratch[0] = jnp.where(outer, p0[...], p1[...])
        scratch[1] = jnp.where(outer, p3, p2[...])
        mine = pl.ds(pl.multiple_of(zl * count, count), count)
        other = pl.ds(pl.multiple_of((1 - zl) * count, count), count)
        for n in range(2):
            keep[pl.ds(n * count, count), :] = scratch[n, mine, :]
            send[pl.ds(n * count, count), :] = scratch[n, other, :]

    return call(
        last,
        [(own.shape, bf16)] * 2,
        [V] * 8,
        [pltpu.VMEM((2,) + own.shape, bf16)],
        moved=20 * own.size,
    )(own, *received, residual, *stored)


def leave(keep, received, batches):
    count, columns = keep.shape[0] // 2, keep.shape[1]
    size = count // batches

    def kernel(a, b, down, up):
        first = lax.axis_index("section") < 2
        value = a[...].astype(f32) + b[...].astype(f32)
        one, two = value[:count], value[count:]
        for out, rows in ((down, jnp.where(first, one, two)), (up, jnp.where(first, two, one))):
            for batch in range(batches):
                out[0, batch] = rows[batch * size : (batch + 1) * size].astype(bf16)

    return call(
        kernel, [((1, batches, size, columns), bf16)] * 2, [V] * 2, moved=8 * keep.size
    )(keep, received)


def pair_sum(a, b):
    def kernel(p, q, *outs):
        value = (p[...].astype(f32) + q[...].astype(f32)).astype(bf16)
        for out in outs:
            out[...] = value

    return call(kernel, [(a.shape, bf16)] * X, [V] * 2, moved=6 * a.size)(a, b)


def local(
    down_input, up_input, down_gain, down_gate, down_up, down_proj, up_gain, up_gate, up_up, up_proj
):
    features = down_input.shape[2] * TENSOR
    gains = (down_gain, up_gain)
    gates, ups, projs = (down_gate, up_gate), (down_up, up_up), (down_proj, up_proj)
    stored = []
    for tick in range(4):
        early = tick < 2
        if tick == 0:
            *parts, residual = enter((down_input, up_input), gains, gates, ups)
        else:
            parts = gate_up(xs, gains, gates, ups, early)
        hidden = hidden_of(exchanged(parts), features)
        hidden = exchanged(hidden)
        other = along(down_part(hidden, projs, early, 1, bf16), "dp", CORE_PAIRS)
        own, *sends = add_and_split(down_part(hidden, projs, early, 0, f32), other)
        received = [along(s, "dp", x_pairs(k + 1)) for k, s in enumerate(sends)]
        if tick == 3:
            keep, send = partial_sum(own, received, residual, stored)
            return leave(keep, along(send, "dp", ZL_PAIRS), down_input.shape[0])
        near, far, kept = partial_sum(own, received, residual)
        stored.append(kept)
        near = along(near, ("dp", "section"), section_pairs(MOVES[tick], 0))
        far = along(far, ("dp", "section"), section_pairs(MOVES[tick], 2))
        residual, *copies = pair_sum(near, far)
        half = [residual] + [along(c, "dp", x_pairs(k + 1)) for k, c in enumerate(copies)]
        half = jnp.concatenate(half, axis=0)
        xs = [half, along(half, "dp", CORE_PAIRS)]


def solution(mesh):
    placed = (
        P(None, None, "tensor"),
        P(None, None, "tensor"),
        P("section", "tensor"),
        P("section", "tensor", "dp"),
        P("section", "tensor", "dp"),
        P("section", "dp", "tensor"),
        P("section", "tensor"),
        P("section", "tensor", "dp"),
        P("section", "tensor", "dp"),
        P("section", "dp", "tensor"),
    )
    return jax.shard_map(
        local,
        mesh=mesh,
        in_specs=placed,
        out_specs=(P("section", None, "dp", "tensor"), P("section", None, "dp", "tensor")),
        check_vma=False,
    )
```

```python
import jax
import jax.numpy as jnp
from jax import lax
from jax.experimental import pallas as pl
from jax.experimental.pallas import tpu as pltpu
from jax.sharding import PartitionSpec as P

EPSILON = 1e-05
X, ZL, CORE, TENSOR = 4, 2, 2, 4
VMEM_LIMIT = 20 * 1024 * 1024
ENTER_LIMIT = 59 * 1024 * 1024
f32, bf16 = jnp.float32, jnp.bfloat16


def along(value, axis, pairs):
    return lax.ppermute(value, axis, pairs)


def tensor_pairs(k):
    return [(i, i ^ k) for i in range(TENSOR)]


def exchanged(shares):
    return [shares[0]] + [
        along(share, "tensor", tensor_pairs(k)) for k, share in zip(TENSOR_ORDER, shares[1:])
    ]


def x_pairs(steps):
    return [(i, (i + 4 * steps) % 16) for i in range(16)]


TENSOR_ORDER = (1, 3, 2)
SHARE = 32
CORE_PAIRS = [(i, i ^ 1) for i in range(16)]
ZL_PAIRS = [(i, i ^ 2) for i in range(16)]


def section_pairs(moves, flip):
    return [(d * 4 + a, (d ^ flip) * 4 + b) for d in range(16) for a, b in moves]


OUTER = [(0, 1), (1, 0), (2, 3), (3, 2)]
MOVES = (OUTER, [(1, 2), (2, 1), (0, 3), (3, 0)], OUTER)


def call(kernel, outs, ins, scratch=(), flops=0, moved=0, grant=VMEM_LIMIT):
    return pl.pallas_call(
        kernel,
        out_shape=[jax.ShapeDtypeStruct(s, d) for s, d in outs],
        in_specs=ins,
        out_specs=[pl.BlockSpec(memory_space=pltpu.VMEM)] * len(outs),
        scratch_shapes=list(scratch),
        compiler_params=pltpu.CompilerParams(vmem_limit_bytes=grant),
        cost_estimate=pl.CostEstimate(flops=flops, bytes_accessed=moved, transcendentals=0),
    )


V = pl.BlockSpec(memory_space=pltpu.VMEM)
A = pl.BlockSpec(memory_space=pl.ANY)
H = pl.BlockSpec(memory_space=pltpu.HBM)


def chosen(early):
    return (lax.axis_index("section") < 2) == early


def fetch(early, pairs, sems):
    down = chosen(early)

    @pl.when(down)
    def _():
        for n, (first, _, target) in enumerate(pairs):
            pltpu.make_async_copy(first, target, sems.at[n]).start()

    @pl.when(jnp.logical_not(down))
    def _():
        for n, (_, second, target) in enumerate(pairs):
            pltpu.make_async_copy(second, target, sems.at[n]).start()


def normalise(v, gain, rows, extra):
    me = lax.axis_index("tensor")
    lane = lax.broadcasted_iota(jnp.int32, (1, 128), 1)
    for start in range(0, v.shape[0], SHARE):
        half, share = divmod(start // SHARE, TENSOR)
        part = v[start : start + SHARE]
        place = half * TENSOR + lax.bitwise_xor(me, share)
        at = pl.ds(pl.multiple_of(place * SHARE, SHARE), SHARE)
        rows[at, :] = (part * gain).astype(bf16)
        total = jnp.sum(part * part, axis=1, keepdims=True)
        high = total.astype(bf16).astype(f32)
        extra[at, :] = jnp.where(lane < 64, high, total - high).astype(bf16)


def share_products(rows, extra, weights, outs, wait=None):
    width = weights[0].shape[1]
    starts = [
        (half * TENSOR + k) * SHARE
        for half in range(len(outs) // TENSOR)
        for k in (0,) + TENSOR_ORDER
    ]
    outs = tuple(zip(starts, outs))
    for start, out in outs:
        out[:, pl.ds(2 * width, 128)] = extra[pl.ds(start, SHARE), :]
    for part, w in enumerate(weights):
        if wait is not None:
            wait(part)
        product = jnp.dot(rows[...], w[...], preferred_element_type=f32).astype(bf16)
        for start, out in outs:
            out[:, pl.ds(part * width, width)] = product[start : start + SHARE]


def enter(inputs, gains, gates, ups):
    batches, tokens, depth = inputs[0].shape
    width = gates[0].shape[2]
    total, per_data = batches * tokens, tokens // 16
    chunk = total // (CORE * X)

    def kernel(di, ui, gd, gu, dg, ug, du, uu, *refs):
        outs, (res, wg, wu, xin, xf, xr, rows, extra, sems) = refs[: CORE * TENSOR], refs[CORE * TENSOR :]
        fetch(True, ((di, ui, xin), (dg.at[0], ug.at[0], wg), (du.at[0], uu.at[0], wu)), sems)
        gain = jnp.where(chosen(True), gd[...].astype(f32), gu[...].astype(f32))
        pltpu.make_async_copy(di, xin, sems.at[0]).wait()
        for batch in range(batches):
            xf[pl.ds(batch * tokens, tokens), :] = xin[batch].astype(f32)
        dp = lax.axis_index("dp")
        x_at, core_at = dp // (ZL * CORE), lax.rem(dp, CORE)
        for c in range(CORE):
            core = core_at if c == 0 else 1 - core_at
            for j in range(X):
                group = lax.rem(x_at + X - j, X) * (ZL * CORE) + core
                for zl in range(ZL):
                    for batch in range(batches):
                        source = pl.multiple_of(batch * tokens + (group + zl * CORE) * per_data, per_data)
                        target = (((c * X + j) * ZL + zl) * batches + batch) * per_data
                        xr[pl.ds(target, per_data), :] = xf[pl.ds(source, per_data), :]
        normalise(xr[...], gain, rows, extra)
        res[...] = xr[pl.ds(0, chunk), :].astype(bf16)

        def wait(part):
            pltpu.make_async_copy((dg, du)[part].at[0], (wg, wu)[part], sems.at[1 + part]).wait()

        share_products(rows, extra, (wg, wu), outs, wait)

    return call(
        kernel,
        [((SHARE, 2 * width + 128), bf16)] * (CORE * TENSOR) + [((chunk, depth), bf16)],
        [H] * 2 + [V] * 2 + [H] * 4,
        [
            pltpu.VMEM((depth, width), bf16),
            pltpu.VMEM((depth, width), bf16),
            pltpu.VMEM((batches, tokens, depth), bf16),
            pltpu.VMEM((total, depth), f32),
            pltpu.VMEM((total, depth), f32),
            pltpu.VMEM((total, depth), bf16),
            pltpu.VMEM((total, 128), bf16),
            pltpu.SemaphoreType.DMA((3,)),
        ],
        flops=4 * total * depth * width,
        moved=6 * depth * width,
        grant=ENTER_LIMIT,
    )(*inputs, *gains, *gates, *ups)


def gate_up(x, gains, gates, ups, early, after=()):
    tokens = x.shape[0]
    depth, width = gates[0].shape[1:]

    def kernel(x, gd, gu, dg, ug, du, uu, *refs):
        outs, (rows, extra) = refs[len(after) : len(after) + TENSOR], refs[len(after) + TENSOR :]
        down = chosen(early)
        gain = jnp.where(down, gd[...].astype(f32), gu[...].astype(f32))
        normalise(x[...].astype(f32), gain, rows, extra)

        @pl.when(down)
        def _():
            share_products(rows, extra, (dg.at[0], du.at[0]), outs)

        @pl.when(jnp.logical_not(down))
        def _():
            share_products(rows, extra, (ug.at[0], uu.at[0]), outs)

    return call(
        kernel,
        [((SHARE, 2 * width + 128), bf16)] * TENSOR,
        [V] * 7 + [A] * len(after),
        [pltpu.VMEM((tokens, depth), bf16), pltpu.VMEM((tokens, 128), bf16)],
        flops=4 * tokens * depth * width,
        moved=4 * depth * width,
    )(x, *gains, *gates, *ups, *after)


def hidden_of(parts, features, after=()):
    count, width = parts[0].shape[0], (parts[0].shape[1] - 128) // 2

    def kernel(a, b, c, d, *outs):
        refs, outs = (a, b, c, d), outs[len(after) :]
        tail = sum(r[:, pl.ds(2 * width, 128)].astype(f32) for r in refs)
        squares = tail[:, 0:1] + tail[:, 64:65]
        inverse = lax.rsqrt(squares / features + EPSILON)
        gate = sum(r[:, pl.ds(0, width)].astype(f32) for r in refs) * inverse
        up = sum(r[:, pl.ds(width, width)].astype(f32) for r in refs) * inverse
        value = (gate / (1.0 + jnp.exp(-gate)) * up).astype(bf16)
        for out in outs:
            out[...] = value

    return call(kernel, [((count, width), bf16)] * TENSOR, [V] * 4 + [A] * len(after), moved=8 * count * width)(*parts, *after)


def down_part(hidden, projs, early, dtype, after=()):
    width = hidden[0].shape[1]
    columns = projs[0].shape[2]
    half = SHARE * TENSOR

    def kernel(h0, h1, h2, h3, first, second, *refs):
        out, rows = refs[len(after) :]
        me = lax.axis_index("tensor")
        for k, share in zip((0,) + TENSOR_ORDER, (h0, h1, h2, h3)):
            at = pl.multiple_of(lax.bitwise_xor(me, k) * SHARE, SHARE)
            rows[pl.ds(at, SHARE), :] = share[...]
        down = chosen(early)

        @pl.when(down)
        def _():
            out[...] = jnp.dot(rows[...], first[0], preferred_element_type=f32).astype(dtype)

        @pl.when(jnp.logical_not(down))
        def _():
            out[...] = jnp.dot(rows[...], second[0], preferred_element_type=f32).astype(dtype)

    return call(
        kernel,
        [((half, columns), dtype)],
        [V] * 6 + [A] * len(after),
        [pltpu.VMEM((half, width), bf16)],
        flops=2 * half * width * columns,
        moved=2 * width * columns,
    )(*hidden, *projs, *after)[0]


def add_and_split(keep, received):
    rows, columns = keep.shape
    chunk = rows // X

    def kernel(a, b, own, s1, s2, s3):
        own[...] = a[pl.ds(0, chunk), :] + b[pl.ds(0, chunk), :].astype(f32)
        for k, out in ((1, s1), (2, s2), (3, s3)):
            at = pl.ds((X - k) * chunk, chunk)
            out[...] = (a[at, :] + b[at, :].astype(f32)).astype(bf16)

    return call(
        kernel, [((chunk, columns), f32)] + [((chunk, columns), bf16)] * 3, [V] * 2, moved=6 * rows * columns
    )(keep, received)


def partial_sum(own, received, residual, stored=None):
    def total(a, r1, r2, r3, x):
        zl = lax.rem(lax.axis_index("dp") // CORE, ZL)
        value = a[...] + r1[...].astype(f32) + r2[...].astype(f32) + r3[...].astype(f32)
        return zl, (value + jnp.where(zl == 0, x[...].astype(f32), 0.0)).astype(bf16)

    if stored is None:

        def kernel(a, r1, r2, r3, x, near, far, kept):
            value = total(a, r1, r2, r3, x)[1]
            near[...] = value
            far[...] = value
            kept[...] = value

        return call(kernel, [(own.shape, bf16)] * 3, [V] * 5, moved=12 * own.size)(own, *received, residual)

    count = own.shape[0] // ZL

    def last(a, r1, r2, r3, x, p0, p1, p2, keep, send, scratch):
        zl, p3 = total(a, r1, r2, r3, x)
        section = lax.axis_index("section")
        outer = jnp.logical_or(section == 0, section == 3)
        scratch[0] = jnp.where(outer, p0[...], p1[...])
        scratch[1] = jnp.where(outer, p3, p2[...])
        mine = pl.ds(pl.multiple_of(zl * count, count), count)
        other = pl.ds(pl.multiple_of((1 - zl) * count, count), count)
        for n in range(2):
            keep[pl.ds(n * count, count), :] = scratch[n, mine, :]
            send[pl.ds(n * count, count), :] = scratch[n, other, :]

    return call(
        last,
        [(own.shape, bf16)] * 2,
        [V] * 8,
        [pltpu.VMEM((2,) + own.shape, bf16)],
        moved=20 * own.size,
    )(own, *received, residual, *stored)


def leave(keep, received, batches):
    count, columns = keep.shape[0] // 2, keep.shape[1]
    size = count // batches

    def kernel(a, b, down, up):
        first = lax.axis_index("section") < 2
        value = a[...].astype(f32) + b[...].astype(f32)
        one, two = value[:count], value[count:]
        for out, rows in ((down, jnp.where(first, one, two)), (up, jnp.where(first, two, one))):
            for batch in range(batches):
                out[0, batch] = rows[batch * size : (batch + 1) * size].astype(bf16)

    return call(
        kernel, [((1, batches, size, columns), bf16)] * 2, [V] * 2, moved=8 * keep.size
    )(keep, received)


def pair_sum(a, b):
    def kernel(p, q, *outs):
        value = (p[...].astype(f32) + q[...].astype(f32)).astype(bf16)
        for out in outs:
            out[...] = value

    return call(kernel, [(a.shape, bf16)] * X, [V] * 2, moved=6 * a.size)(a, b)


def local(
    down_input, up_input, down_gain, down_gate, down_up, down_proj, up_gain, up_gate, up_up, up_proj
):
    features = down_input.shape[2] * TENSOR
    gains = (down_gain, up_gain)
    gates, ups, projs = (down_gate, up_gate), (down_up, up_up), (down_proj, up_proj)
    stored = []
    for tick in range(4):
        early = tick < 2
        if tick == 0:
            *parts, residual = enter((down_input, up_input), gains, gates, ups)
        else:
            parts = gate_up(half, gains, gates, ups, early)
            parts = parts + gate_up(rest, gains, gates, ups, early, parts[:1])
        kept = hidden_of(exchanged(parts[:TENSOR]), features)
        lent = hidden_of(exchanged(parts[TENSOR:]), features, kept[:1])
        kept, lent = exchanged(kept), exchanged(lent)
        kept = down_part(kept, projs, early, f32)
        other = along(down_part(lent, projs, early, bf16, (kept,)), "dp", CORE_PAIRS)
        own, *sends = add_and_split(kept, other)
        received = [along(s, "dp", x_pairs(k + 1)) for k, s in enumerate(sends)]
        if tick == 3:
            keep, send = partial_sum(own, received, residual, stored)
            return leave(keep, along(send, "dp", ZL_PAIRS), down_input.shape[0])
        near, far, kept = partial_sum(own, received, residual)
        stored.append(kept)
        near = along(near, ("dp", "section"), section_pairs(MOVES[tick], 0))
        far = along(far, ("dp", "section"), section_pairs(MOVES[tick], 2))
        residual, *copies = pair_sum(near, far)
        half = [residual] + [along(c, "dp", x_pairs(k + 1)) for k, c in enumerate(copies)]
        half = jnp.concatenate(half, axis=0)
        rest = along(half, "dp", CORE_PAIRS)


def solution(mesh):
    placed = (
        P(None, None, "tensor"),
        P(None, None, "tensor"),
        P("section", "tensor"),
        P("section", "tensor", "dp"),
        P("section", "tensor", "dp"),
        P("section", "dp", "tensor"),
        P("section", "tensor"),
        P("section", "tensor", "dp"),
        P("section", "tensor", "dp"),
        P("section", "dp", "tensor"),
    )
    return jax.shard_map(
        local,
        mesh=mesh,
        in_specs=placed,
        out_specs=(P("section", None, "dp", "tensor"), P("section", None, "dp", "tensor")),
        check_vma=False,
    )
```

```python
import jax
import jax.numpy as jnp
from jax import lax
from jax.experimental import pallas as pl
from jax.experimental.pallas import tpu as pltpu
from jax.sharding import PartitionSpec as P

EPSILON = 1e-05
X, ZL, CORE, TENSOR = 4, 2, 2, 4
VMEM_LIMIT = 20 * 1024 * 1024
ENTER_LIMIT = 59 * 1024 * 1024
WEIGHT = 40
f32, bf16 = jnp.float32, jnp.bfloat16


def along(value, axis, pairs):
    return lax.ppermute(value, axis, pairs)


def tensor_pairs(k):
    return [(i, i ^ k) for i in range(TENSOR)]


def exchanged(shares):
    return [shares[0]] + [
        along(share, "tensor", tensor_pairs(k)) for k, share in zip(TENSOR_ORDER, shares[1:])
    ]


def x_pairs(steps):
    return [(i, (i + 4 * steps) % 16) for i in range(16)]


TENSOR_ORDER = (1, 3, 2)
SHARE = 32
CORE_PAIRS = [(i, i ^ 1) for i in range(16)]
ZL_PAIRS = [(i, i ^ 2) for i in range(16)]


def section_pairs(moves, flip):
    return [(d * 4 + a, (d ^ flip) * 4 + b) for d in range(16) for a, b in moves]


OUTER = [(0, 1), (1, 0), (2, 3), (3, 2)]
MOVES = (OUTER, [(1, 2), (2, 1), (0, 3), (3, 0)], OUTER)


def call(kernel, outs, ins, scratch=(), flops=0, moved=0, grant=VMEM_LIMIT):
    return pl.pallas_call(
        kernel,
        out_shape=[jax.ShapeDtypeStruct(s, d) for s, d in outs],
        in_specs=ins,
        out_specs=[pl.BlockSpec(memory_space=pltpu.VMEM)] * len(outs),
        scratch_shapes=list(scratch),
        compiler_params=pltpu.CompilerParams(vmem_limit_bytes=grant),
        cost_estimate=pl.CostEstimate(flops=flops, bytes_accessed=moved, transcendentals=0),
    )


V = pl.BlockSpec(memory_space=pltpu.VMEM)
A = pl.BlockSpec(memory_space=pl.ANY)
H = pl.BlockSpec(memory_space=pltpu.HBM)


def chosen(early):
    return (lax.axis_index("section") < 2) == early


def fetch(early, pairs, sems):
    down = chosen(early)

    @pl.when(down)
    def _():
        for n, (first, _, target) in enumerate(pairs):
            pltpu.make_async_copy(first, target, sems.at[n]).start()

    @pl.when(jnp.logical_not(down))
    def _():
        for n, (_, second, target) in enumerate(pairs):
            pltpu.make_async_copy(second, target, sems.at[n]).start()


def normalise(v, gain, rows, extra):
    me = lax.axis_index("tensor")
    lane = lax.broadcasted_iota(jnp.int32, (1, 128), 1)
    for start in range(0, v.shape[0], SHARE):
        half, share = divmod(start // SHARE, TENSOR)
        part = v[start : start + SHARE]
        place = half * TENSOR + lax.bitwise_xor(me, share)
        at = pl.ds(pl.multiple_of(place * SHARE, SHARE), SHARE)
        rows[at, :] = (part * gain).astype(bf16)
        total = jnp.sum(part * part, axis=1, keepdims=True)
        high = total.astype(bf16).astype(f32)
        extra[at, :] = jnp.where(lane < 64, high, total - high).astype(bf16)


def share_products(rows, extra, weights, outs, wait=None):
    width = weights[0].shape[1]
    starts = [
        (half * TENSOR + k) * SHARE
        for half in range(len(outs) // TENSOR)
        for k in (0,) + TENSOR_ORDER
    ]
    outs = tuple(zip(starts, outs))
    for start, out in outs:
        out[:, pl.ds(2 * width, 128)] = extra[pl.ds(start, SHARE), :]
    for part, w in enumerate(weights):
        if wait is not None:
            wait(part)
        product = jnp.dot(rows[...], w[...], preferred_element_type=f32).astype(bf16)
        for start, out in outs:
            out[:, pl.ds(part * width, width)] = product[start : start + SHARE]


def enter(inputs, gains, gates, ups):
    batches, tokens, depth = inputs[0].shape
    width = gates[0].shape[2]
    total, per_data = batches * tokens, tokens // 16
    chunk = total // (CORE * X)

    def kernel(di, ui, gd, gu, dg, ug, du, uu, *refs):
        outs, (res, wg, wu, xin, xf, xr, rows, extra, sems) = refs[: CORE * TENSOR], refs[CORE * TENSOR :]
        fetch(True, ((di, ui, xin), (dg.at[0], ug.at[0], wg), (du.at[0], uu.at[0], wu)), sems)
        gain = jnp.where(chosen(True), gd[...].astype(f32), gu[...].astype(f32))
        pltpu.make_async_copy(di, xin, sems.at[0]).wait()
        for batch in range(batches):
            xf[pl.ds(batch * tokens, tokens), :] = xin[batch].astype(f32)
        dp = lax.axis_index("dp")
        x_at, core_at = dp // (ZL * CORE), lax.rem(dp, CORE)
        for c in range(CORE):
            core = core_at if c == 0 else 1 - core_at
            for j in range(X):
                group = lax.rem(x_at + X - j, X) * (ZL * CORE) + core
                for zl in range(ZL):
                    for batch in range(batches):
                        source = pl.multiple_of(batch * tokens + (group + zl * CORE) * per_data, per_data)
                        target = (((c * X + j) * ZL + zl) * batches + batch) * per_data
                        xr[pl.ds(target, per_data), :] = xf[pl.ds(source, per_data), :]
        normalise(xr[...], gain, rows, extra)
        res[...] = xr[pl.ds(X * chunk, chunk), :].astype(bf16)

        def wait(part):
            pltpu.make_async_copy((dg, du)[part].at[0], (wg, wu)[part], sems.at[1 + part]).wait()

        share_products(rows, extra, (wg, wu), outs, wait)

    return call(
        kernel,
        [((SHARE, 2 * width + 128), bf16)] * (CORE * TENSOR) + [((chunk, depth), bf16)],
        [H] * 2 + [V] * 2 + [H] * 4,
        [
            pltpu.VMEM((depth, width), bf16),
            pltpu.VMEM((depth, width), bf16),
            pltpu.VMEM((batches, tokens, depth), bf16),
            pltpu.VMEM((total, depth), f32),
            pltpu.VMEM((total, depth), f32),
            pltpu.VMEM((total, depth), bf16),
            pltpu.VMEM((total, 128), bf16),
            pltpu.SemaphoreType.DMA((3,)),
        ],
        flops=4 * total * depth * width,
        moved=6 * depth * width,
        grant=ENTER_LIMIT,
    )(*inputs, *gains, *gates, *ups)


def gate_up(x, gains, gates, ups, early, after=()):
    tokens = x.shape[0]
    depth, width = gates[0].shape[1:]

    def kernel(x, gd, gu, dg, ug, du, uu, *refs):
        outs, (rows, extra) = refs[len(after) : len(after) + TENSOR], refs[len(after) + TENSOR :]
        down = chosen(early)
        gain = jnp.where(down, gd[...].astype(f32), gu[...].astype(f32))
        normalise(x[...].astype(f32), gain, rows, extra)

        @pl.when(down)
        def _():
            share_products(rows, extra, (dg.at[0], du.at[0]), outs)

        @pl.when(jnp.logical_not(down))
        def _():
            share_products(rows, extra, (ug.at[0], uu.at[0]), outs)

    return call(
        kernel,
        [((SHARE, 2 * width + 128), bf16)] * TENSOR,
        [V] * 7 + [A] * len(after),
        [pltpu.VMEM((tokens, depth), bf16), pltpu.VMEM((tokens, 128), bf16)],
        flops=4 * tokens * depth * width,
        moved=4 * depth * width,
    )(x, *gains, *gates, *ups, *after)


def hidden_of(parts, features, after=()):
    count, width = parts[0].shape[0], (parts[0].shape[1] - 128) // 2

    def kernel(a, b, c, d, *outs):
        refs, outs = (a, b, c, d), outs[len(after) :]
        tail = sum(r[:, pl.ds(2 * width, 128)].astype(f32) for r in refs)
        squares = tail[:, 0:1] + tail[:, 64:65]
        inverse = lax.rsqrt(squares / features + EPSILON)
        gate = sum(r[:, pl.ds(0, width)].astype(f32) for r in refs) * inverse
        up = sum(r[:, pl.ds(width, width)].astype(f32) for r in refs) * inverse
        value = (gate / (1.0 + jnp.exp(-gate)) * up).astype(bf16)
        for out in outs:
            out[...] = value

    return call(kernel, [((count, width), bf16)] * TENSOR, [V] * 4 + [A] * len(after), moved=8 * count * width)(*parts, *after)


def down_part(hidden, projs, early, dtype, after=(), weight=1):
    width = hidden[0].shape[1]
    columns = projs[0].shape[2]
    half = SHARE * TENSOR

    def kernel(h0, h1, h2, h3, first, second, *refs):
        out, rows = refs[len(after) :]
        me = lax.axis_index("tensor")
        for k, share in zip((0,) + TENSOR_ORDER, (h0, h1, h2, h3)):
            at = pl.multiple_of(lax.bitwise_xor(me, k) * SHARE, SHARE)
            rows[pl.ds(at, SHARE), :] = share[...]
        down = chosen(early)

        @pl.when(down)
        def _():
            out[...] = jnp.dot(rows[...], first[0], preferred_element_type=f32).astype(dtype)

        @pl.when(jnp.logical_not(down))
        def _():
            out[...] = jnp.dot(rows[...], second[0], preferred_element_type=f32).astype(dtype)

    return call(
        kernel,
        [((half, columns), dtype)],
        [V] * 6 + [A] * len(after),
        [pltpu.VMEM((half, width), bf16)],
        flops=2 * half * width * columns * weight,
        moved=2 * width * columns * weight,
    )(*hidden, *projs, *after)[0]


def add_and_split(keep, received):
    rows, columns = keep.shape
    chunk = rows // X

    def kernel(a, b, own, s1, s2, s3):
        own[...] = a[pl.ds(0, chunk), :] + b[pl.ds(0, chunk), :].astype(f32)
        for k, out in ((1, s1), (2, s2), (3, s3)):
            at = pl.ds((X - k) * chunk, chunk)
            out[...] = (a[at, :] + b[at, :].astype(f32)).astype(bf16)

    return call(
        kernel, [((chunk, columns), f32)] + [((chunk, columns), bf16)] * 3, [V] * 2, moved=6 * rows * columns
    )(keep, received)


def partial_sum(own, received, residual, stored=None):
    def total(a, r1, r2, r3, x):
        zl = lax.rem(lax.axis_index("dp") // CORE, ZL)
        value = a[...] + r1[...].astype(f32) + r2[...].astype(f32) + r3[...].astype(f32)
        value = value + jnp.where(zl == 0, x[pl.ds(0, a.shape[0]), :].astype(f32), 0.0)
        return zl, value.astype(bf16)

    if stored is None:

        def kernel(a, r1, r2, r3, x, near, far, kept):
            value = total(a, r1, r2, r3, x)[1]
            near[...] = value
            far[...] = value
            kept[...] = value

        return call(kernel, [(own.shape, bf16)] * 3, [V] * 5, moved=12 * own.size)(own, *received, residual)

    count = own.shape[0] // ZL

    def last(a, r1, r2, r3, x, p1, other, keep, send, scratch):
        zl, p3 = total(a, r1, r2, r3, x)
        section = lax.axis_index("section")
        outer = jnp.logical_or(section == 0, section == 3)
        scratch[0] = jnp.where(outer, other[...], p1[...])
        scratch[1] = jnp.where(outer, p3, other[...])
        mine = pl.ds(pl.multiple_of(zl * count, count), count)
        other = pl.ds(pl.multiple_of((1 - zl) * count, count), count)
        for n in range(2):
            keep[pl.ds(n * count, count), :] = scratch[n, mine, :]
            send[pl.ds(n * count, count), :] = scratch[n, other, :]

    return call(
        last,
        [(own.shape, bf16)] * 2,
        [V] * 7,
        [pltpu.VMEM((2,) + own.shape, bf16)],
        moved=20 * own.size,
    )(own, *received, residual, *stored)


def leave(keep, received, batches):
    count, columns = keep.shape[0] // 2, keep.shape[1]
    size = count // batches

    def kernel(a, b, down, up):
        first = lax.axis_index("section") < 2
        value = a[...].astype(f32) + b[...].astype(f32)
        one, two = value[:count], value[count:]
        for out, rows in ((down, jnp.where(first, one, two)), (up, jnp.where(first, two, one))):
            for batch in range(batches):
                out[0, batch] = rows[batch * size : (batch + 1) * size].astype(bf16)

    return call(
        kernel, [((1, batches, size, columns), bf16)] * 2, [V] * 2, moved=8 * keep.size
    )(keep, received)


def pair_sum(a, b):
    def kernel(p, q, *outs):
        value = (p[...].astype(f32) + q[...].astype(f32)).astype(bf16)
        for out in outs:
            out[...] = value

    return call(kernel, [(a.shape, bf16)] * X, [V] * 2, moved=6 * a.size)(a, b)


def local(
    down_input, up_input, down_gain, down_gate, down_up, down_proj, up_gain, up_gate, up_up, up_proj
):
    features = down_input.shape[2] * TENSOR
    gains = (down_gain, up_gain)
    gates, ups, projs = (down_gate, up_gate), (down_up, up_up), (down_proj, up_proj)
    stored = []
    for tick in range(4):
        early = tick < 2
        if tick == 0:
            *parts, residual = enter((down_input, up_input), gains, gates, ups)
        else:
            parts = gate_up(half, gains, gates, ups, early)
            parts = parts + gate_up(rest, gains, gates, ups, early, parts[:1])
        lent = hidden_of(exchanged(parts[:TENSOR]), features, parts[TENSOR : TENSOR + 1])
        kept = hidden_of(exchanged(parts[TENSOR:]), features, lent[:1])
        made = kept[0]
        lent, kept = exchanged(lent), exchanged(kept)
        lent = down_part(lent, projs, early, bf16, (made,))
        kept = down_part(kept, projs, early, f32, (lent,), WEIGHT)
        own, *sends = add_and_split(kept, along(lent, "dp", CORE_PAIRS))
        received = [along(s, "dp", x_pairs(k + 1)) for k, s in enumerate(sends)]
        if tick == 3:
            outer = (lax.axis_index("section") % 3) == 0
            crossed = along(jnp.where(outer, stored[0], stored[2]), "dp", CORE_PAIRS)
            keep, send = partial_sum(own, received, residual, (stored[1], crossed))
            return leave(keep, along(send, "dp", ZL_PAIRS), down_input.shape[0])
        near, far, kept = partial_sum(own, received, residual)
        stored.append(kept)
        near = along(near, ("dp", "section"), section_pairs(MOVES[tick], 0))
        far = along(far, ("dp", "section"), section_pairs(MOVES[tick], 2))
        chunk, *copies = pair_sum(near, far)
        half = [chunk] + [along(c, "dp", x_pairs(k + 1)) for k, c in enumerate(copies)]
        half = jnp.concatenate(half, axis=0)
        residual = rest = along(half, "dp", CORE_PAIRS)


def solution(mesh):
    placed = (
        P(None, None, "tensor"),
        P(None, None, "tensor"),
        P("section", "tensor"),
        P("section", "tensor", "dp"),
        P("section", "tensor", "dp"),
        P("section", "dp", "tensor"),
        P("section", "tensor"),
        P("section", "tensor", "dp"),
        P("section", "tensor", "dp"),
        P("section", "dp", "tensor"),
    )
    return jax.shard_map(
        local,
        mesh=mesh,
        in_specs=placed,
        out_specs=(P("section", None, "dp", "tensor"), P("section", None, "dp", "tensor")),
        check_vma=False,
    )
```

```python
import jax
import jax.numpy as jnp
from jax import lax
from jax.experimental import pallas as pl
from jax.experimental.pallas import tpu as pltpu
from jax.sharding import PartitionSpec as P

EPSILON = 1e-05
X, ZL, CORE, TENSOR = 4, 2, 2, 4
VMEM_LIMIT = 20 * 1024 * 1024
ENTER_LIMIT = 59 * 1024 * 1024
WEIGHT = 40
f32, bf16 = jnp.float32, jnp.bfloat16


def along(value, axis, pairs):
    return lax.ppermute(value, axis, pairs)


def tensor_pairs(k):
    return [(i, i ^ k) for i in range(TENSOR)]


def exchanged(shares):
    return [shares[0]] + [
        along(share, "tensor", tensor_pairs(k)) for k, share in zip(TENSOR_ORDER, shares[1:])
    ]


def x_pairs(steps):
    return [(i, (i + 4 * steps) % 16) for i in range(16)]


TENSOR_ORDER = (1, 3, 2)
SHARE = 32
CORE_PAIRS = [(i, i ^ 1) for i in range(16)]
ZL_PAIRS = [(i, i ^ 2) for i in range(16)]


def section_pairs(moves, flip):
    return [(d * 4 + a, (d ^ flip) * 4 + b) for d in range(16) for a, b in moves]


OUTER = [(0, 1), (1, 0), (2, 3), (3, 2)]
MOVES = (OUTER, [(1, 2), (2, 1), (0, 3), (3, 0)], OUTER)


def call(kernel, outs, ins, scratch=(), flops=0, moved=0, grant=VMEM_LIMIT):
    return pl.pallas_call(
        kernel,
        out_shape=[jax.ShapeDtypeStruct(s, d) for s, d in outs],
        in_specs=ins,
        out_specs=[pl.BlockSpec(memory_space=pltpu.VMEM)] * len(outs),
        scratch_shapes=list(scratch),
        compiler_params=pltpu.CompilerParams(vmem_limit_bytes=grant),
        cost_estimate=pl.CostEstimate(flops=flops, bytes_accessed=moved, transcendentals=0),
    )


V = pl.BlockSpec(memory_space=pltpu.VMEM)
A = pl.BlockSpec(memory_space=pl.ANY)
H = pl.BlockSpec(memory_space=pltpu.HBM)


def chosen(early):
    return (lax.axis_index("section") < 2) == early


def fetch(early, pairs, sems):
    down = chosen(early)

    @pl.when(down)
    def _():
        for n, (first, _, target) in enumerate(pairs):
            pltpu.make_async_copy(first, target, sems.at[n]).start()

    @pl.when(jnp.logical_not(down))
    def _():
        for n, (_, second, target) in enumerate(pairs):
            pltpu.make_async_copy(second, target, sems.at[n]).start()


def normalise(v, gain, rows, extra):
    me = lax.axis_index("tensor")
    lane = lax.broadcasted_iota(jnp.int32, (1, 128), 1)
    for start in range(0, v.shape[0], SHARE):
        half, share = divmod(start // SHARE, TENSOR)
        part = v[start : start + SHARE]
        place = half * TENSOR + lax.bitwise_xor(me, share)
        at = pl.ds(pl.multiple_of(place * SHARE, SHARE), SHARE)
        rows[at, :] = (part * gain).astype(bf16)
        total = jnp.sum(part * part, axis=1, keepdims=True)
        high = total.astype(bf16).astype(f32)
        extra[at, :] = jnp.where(lane < 64, high, total - high).astype(bf16)


def share_products(rows, extra, weights, outs, wait=None):
    width = weights[0].shape[1]
    starts = [
        (half * TENSOR + k) * SHARE
        for half in range(len(outs) // TENSOR)
        for k in (0,) + TENSOR_ORDER
    ]
    outs = tuple(zip(starts, outs))
    for start, out in outs:
        out[:, pl.ds(2 * width, 128)] = extra[pl.ds(start, SHARE), :]
    for part, w in enumerate(weights):
        if wait is not None:
            wait(part)
        product = jnp.dot(rows[...], w[...], preferred_element_type=f32).astype(bf16)
        for start, out in outs:
            out[:, pl.ds(part * width, width)] = product[start : start + SHARE]


def enter(inputs, gains, gates, ups):
    batches, tokens, depth = inputs[0].shape
    width = gates[0].shape[2]
    total, per_data = batches * tokens, tokens // 16
    chunk = total // (CORE * X)

    def kernel(di, ui, gd, gu, dg, ug, du, uu, *refs):
        own, *others, res, wg, wu, xin, xf, xr, rows, extra, sems = refs
        outs = (own.at[pl.ds(0, SHARE)], *others[: TENSOR - 1])
        outs += (own.at[pl.ds(SHARE, SHARE)], *others[TENSOR - 1 :])
        fetch(True, ((di, ui, xin), (dg.at[0], ug.at[0], wg), (du.at[0], uu.at[0], wu)), sems)
        gain = jnp.where(chosen(True), gd[...].astype(f32), gu[...].astype(f32))
        pltpu.make_async_copy(di, xin, sems.at[0]).wait()
        for batch in range(batches):
            xf[pl.ds(batch * tokens, tokens), :] = xin[batch].astype(f32)
        dp = lax.axis_index("dp")
        x_at, core_at = dp // (ZL * CORE), lax.rem(dp, CORE)
        for c in range(CORE):
            core = core_at if c == 0 else 1 - core_at
            for j in range(X):
                group = lax.rem(x_at + X - j, X) * (ZL * CORE) + core
                for zl in range(ZL):
                    for batch in range(batches):
                        source = pl.multiple_of(batch * tokens + (group + zl * CORE) * per_data, per_data)
                        target = (((c * X + j) * ZL + zl) * batches + batch) * per_data
                        xr[pl.ds(target, per_data), :] = xf[pl.ds(source, per_data), :]
        normalise(xr[...], gain, rows, extra)
        res[...] = xr[pl.ds(X * chunk, chunk), :].astype(bf16)

        def wait(part):
            pltpu.make_async_copy((dg, du)[part].at[0], (wg, wu)[part], sems.at[1 + part]).wait()

        share_products(rows, extra, (wg, wu), outs, wait)

    return call(
        kernel,
        [((CORE * SHARE, 2 * width + 128), bf16)]
        + [((SHARE, 2 * width + 128), bf16)] * (CORE * (TENSOR - 1))
        + [((chunk, depth), bf16)],
        [H] * 2 + [V] * 2 + [H] * 4,
        [
            pltpu.VMEM((depth, width), bf16),
            pltpu.VMEM((depth, width), bf16),
            pltpu.VMEM((batches, tokens, depth), bf16),
            pltpu.VMEM((total, depth), f32),
            pltpu.VMEM((total, depth), f32),
            pltpu.VMEM((total, depth), bf16),
            pltpu.VMEM((total, 128), bf16),
            pltpu.SemaphoreType.DMA((3,)),
        ],
        flops=4 * total * depth * width,
        moved=6 * depth * width,
        grant=ENTER_LIMIT,
    )(*inputs, *gains, *gates, *ups)


def gate_up(x, gains, gates, ups, early, after=()):
    tokens = x.shape[0]
    depth, width = gates[0].shape[1:]

    def kernel(x, gd, gu, dg, ug, du, uu, *refs):
        outs, (rows, extra) = refs[len(after) : len(after) + TENSOR], refs[len(after) + TENSOR :]
        down = chosen(early)
        gain = jnp.where(down, gd[...].astype(f32), gu[...].astype(f32))
        normalise(x[...].astype(f32), gain, rows, extra)

        @pl.when(down)
        def _():
            share_products(rows, extra, (dg.at[0], du.at[0]), outs)

        @pl.when(jnp.logical_not(down))
        def _():
            share_products(rows, extra, (ug.at[0], uu.at[0]), outs)

    return call(
        kernel,
        [((SHARE, 2 * width + 128), bf16)] * TENSOR,
        [V] * 7 + [A] * len(after),
        [pltpu.VMEM((tokens, depth), bf16), pltpu.VMEM((tokens, 128), bf16)],
        flops=4 * tokens * depth * width,
        moved=4 * depth * width,
    )(x, *gains, *gates, *ups, *after)


def hidden_of(parts, features, after=(), row=0):
    count, width = parts[1].shape[0], (parts[0].shape[1] - 128) // 2

    def kernel(a, b, c, d, *outs):
        refs, outs = (a.at[pl.ds(row, count)], b, c, d), outs[len(after) :]
        tail = sum(r[:, pl.ds(2 * width, 128)].astype(f32) for r in refs)
        squares = tail[:, 0:1] + tail[:, 64:65]
        inverse = lax.rsqrt(squares / features + EPSILON)
        gate = sum(r[:, pl.ds(0, width)].astype(f32) for r in refs) * inverse
        up = sum(r[:, pl.ds(width, width)].astype(f32) for r in refs) * inverse
        value = (gate / (1.0 + jnp.exp(-gate)) * up).astype(bf16)
        for out in outs:
            out[...] = value

    return call(kernel, [((count, width), bf16)] * TENSOR, [V] * 4 + [A] * len(after), moved=8 * count * width)(*parts, *after)


def down_part(hidden, projs, early, dtype, after=(), weight=1):
    width = hidden[0].shape[1]
    columns = projs[0].shape[2]
    half = SHARE * TENSOR

    def kernel(h0, h1, h2, h3, first, second, *refs):
        out, rows = refs[len(after) :]
        me = lax.axis_index("tensor")
        for k, share in zip((0,) + TENSOR_ORDER, (h0, h1, h2, h3)):
            at = pl.multiple_of(lax.bitwise_xor(me, k) * SHARE, SHARE)
            rows[pl.ds(at, SHARE), :] = share[...]
        down = chosen(early)

        @pl.when(down)
        def _():
            out[...] = jnp.dot(rows[...], first[0], preferred_element_type=f32).astype(dtype)

        @pl.when(jnp.logical_not(down))
        def _():
            out[...] = jnp.dot(rows[...], second[0], preferred_element_type=f32).astype(dtype)

    return call(
        kernel,
        [((half, columns), dtype)],
        [V] * 6 + [A] * len(after),
        [pltpu.VMEM((half, width), bf16)],
        flops=2 * half * width * columns * weight,
        moved=2 * width * columns * weight,
    )(*hidden, *projs, *after)[0]


def add_and_split(keep, received):
    rows, columns = keep.shape
    chunk = rows // X

    def kernel(a, b, own, s1, s2, s3):
        own[...] = a[pl.ds(0, chunk), :] + b[pl.ds(0, chunk), :].astype(f32)
        for k, out in ((1, s1), (2, s2), (3, s3)):
            at = pl.ds((X - k) * chunk, chunk)
            out[...] = (a[at, :] + b[at, :].astype(f32)).astype(bf16)

    return call(
        kernel, [((chunk, columns), f32)] + [((chunk, columns), bf16)] * 3, [V] * 2, moved=6 * rows * columns
    )(keep, received)


def partial_sum(own, received, residual, stored=None):
    def total(a, r1, r2, r3, x):
        zl = lax.rem(lax.axis_index("dp") // CORE, ZL)
        value = a[...] + r1[...].astype(f32) + r2[...].astype(f32) + r3[...].astype(f32)
        value = value + jnp.where(zl == 0, x[pl.ds(0, a.shape[0]), :].astype(f32), 0.0)
        return zl, value.astype(bf16)

    if stored is None:

        def kernel(a, r1, r2, r3, x, near, far, kept):
            value = total(a, r1, r2, r3, x)[1]
            near[...] = value
            far[...] = value
            kept[...] = value

        return call(kernel, [(own.shape, bf16)] * 3, [V] * 5, moved=12 * own.size)(own, *received, residual)

    count = own.shape[0] // ZL

    def last(a, r1, r2, r3, x, p1, other, keep, send, scratch):
        zl, p3 = total(a, r1, r2, r3, x)
        section = lax.axis_index("section")
        outer = jnp.logical_or(section == 0, section == 3)
        scratch[0] = jnp.where(outer, other[...], p1[...])
        scratch[1] = jnp.where(outer, p3, other[...])
        mine = pl.ds(pl.multiple_of(zl * count, count), count)
        other = pl.ds(pl.multiple_of((1 - zl) * count, count), count)
        for n in range(2):
            keep[pl.ds(n * count, count), :] = scratch[n, mine, :]
            send[pl.ds(n * count, count), :] = scratch[n, other, :]

    return call(
        last,
        [(own.shape, bf16)] * 2,
        [V] * 7,
        [pltpu.VMEM((2,) + own.shape, bf16)],
        moved=20 * own.size,
    )(own, *received, residual, *stored)


def leave(keep, received, batches):
    count, columns = keep.shape[0] // 2, keep.shape[1]
    size = count // batches

    def kernel(a, b, down, up):
        first = lax.axis_index("section") < 2
        value = a[...].astype(f32) + b[...].astype(f32)
        one, two = value[:count], value[count:]
        for out, rows in ((down, jnp.where(first, one, two)), (up, jnp.where(first, two, one))):
            for batch in range(batches):
                out[0, batch] = rows[batch * size : (batch + 1) * size].astype(bf16)

    return call(
        kernel, [((1, batches, size, columns), bf16)] * 2, [V] * 2, moved=8 * keep.size
    )(keep, received)


def pair_sum(a, b):
    def kernel(p, q, *outs):
        value = (p[...].astype(f32) + q[...].astype(f32)).astype(bf16)
        for out in outs:
            out[...] = value

    return call(kernel, [(a.shape, bf16)] * X, [V] * 2, moved=6 * a.size)(a, b)


def local(
    down_input, up_input, down_gain, down_gate, down_up, down_proj, up_gain, up_gate, up_up, up_proj
):
    features = down_input.shape[2] * TENSOR
    gains = (down_gain, up_gain)
    gates, ups, projs = (down_gate, up_gate), (down_up, up_up), (down_proj, up_proj)
    stored = []
    for tick in range(4):
        early = tick < 2
        if tick == 0:
            own, *others, residual = enter((down_input, up_input), gains, gates, ups)
            parts = [own, *others[: TENSOR - 1], own, *others[TENSOR - 1 :]]
        else:
            parts = gate_up(half, gains, gates, ups, early)
            parts = parts + gate_up(rest, gains, gates, ups, early, parts[:1])
        after = parts[TENSOR : TENSOR + 1] if tick else ()
        lent = hidden_of(exchanged(parts[:TENSOR]), features, after)
        kept = hidden_of(exchanged(parts[TENSOR:]), features, lent[:1], 0 if tick else SHARE)
        made = kept[0]
        lent, kept = exchanged(lent), exchanged(kept)
        lent = down_part(lent, projs, early, bf16, (made,))
        kept = down_part(kept, projs, early, f32, (lent,), WEIGHT)
        own, *sends = add_and_split(kept, along(lent, "dp", CORE_PAIRS))
        received = [along(s, "dp", x_pairs(k + 1)) for k, s in enumerate(sends)]
        if tick == 3:
            outer = (lax.axis_index("section") % 3) == 0
            crossed = along(jnp.where(outer, stored[0], stored[2]), "dp", CORE_PAIRS)
            keep, send = partial_sum(own, received, residual, (stored[1], crossed))
            return leave(keep, along(send, "dp", ZL_PAIRS), down_input.shape[0])
        near, far, kept = partial_sum(own, received, residual)
        stored.append(kept)
        near = along(near, ("dp", "section"), section_pairs(MOVES[tick], 0))
        far = along(far, ("dp", "section"), section_pairs(MOVES[tick], 2))
        chunk, *copies = pair_sum(near, far)
        half = [chunk] + [along(c, "dp", x_pairs(k + 1)) for k, c in enumerate(copies)]
        half = jnp.concatenate(half, axis=0)
        residual = rest = along(half, "dp", CORE_PAIRS)


def solution(mesh):
    placed = (
        P(None, None, "tensor"),
        P(None, None, "tensor"),
        P("section", "tensor"),
        P("section", "tensor", "dp"),
        P("section", "tensor", "dp"),
        P("section", "dp", "tensor"),
        P("section", "tensor"),
        P("section", "tensor", "dp"),
        P("section", "tensor", "dp"),
        P("section", "dp", "tensor"),
    )
    return jax.shard_map(
        local,
        mesh=mesh,
        in_specs=placed,
        out_specs=(P("section", None, "dp", "tensor"), P("section", None, "dp", "tensor")),
        check_vma=False,
    )
```

```python
import jax
import jax.numpy as jnp
from jax import lax
from jax.experimental import pallas as pl
from jax.experimental.pallas import tpu as pltpu
from jax.sharding import PartitionSpec as P

EPSILON = 1e-05
X, ZL, CORE, TENSOR = 4, 2, 2, 4
VMEM_LIMIT = 20 * 1024 * 1024
ENTER_LIMIT = 59 * 1024 * 1024
WEIGHT = 40
f32, bf16 = jnp.float32, jnp.bfloat16


def along(value, axis, pairs):
    return lax.ppermute(value, axis, pairs)


def tensor_pairs(k):
    return [(i, i ^ k) for i in range(TENSOR)]


def exchanged(shares):
    return [shares[0]] + [
        along(share, "tensor", tensor_pairs(k)) for k, share in zip(TENSOR_ORDER, shares[1:])
    ]


def x_pairs(k):
    return [(i, i ^ (4 * k)) for i in range(16)]


X_ORDER = (0, 1, 3, 2)
TENSOR_ORDER = (1, 3, 2)
SHARE = 32
CORE_PAIRS = [(i, i ^ 1) for i in range(16)]
ZL_PAIRS = [(i, i ^ 2) for i in range(16)]


def section_pairs(moves, flip):
    return [(d * 4 + a, (d ^ flip) * 4 + b) for d in range(16) for a, b in moves]


OUTER = [(0, 1), (1, 0), (2, 3), (3, 2)]
MOVES = (OUTER, [(1, 2), (2, 1), (0, 3), (3, 0)], OUTER)


def call(kernel, outs, ins, scratch=(), flops=0, moved=0, grant=VMEM_LIMIT):
    return pl.pallas_call(
        kernel,
        out_shape=[jax.ShapeDtypeStruct(s, d) for s, d in outs],
        in_specs=ins,
        out_specs=[pl.BlockSpec(memory_space=pltpu.VMEM)] * len(outs),
        scratch_shapes=list(scratch),
        compiler_params=pltpu.CompilerParams(vmem_limit_bytes=grant),
        cost_estimate=pl.CostEstimate(flops=flops, bytes_accessed=moved, transcendentals=0),
    )


V = pl.BlockSpec(memory_space=pltpu.VMEM)
A = pl.BlockSpec(memory_space=pl.ANY)
H = pl.BlockSpec(memory_space=pltpu.HBM)


def chosen(early):
    return (lax.axis_index("section") < 2) == early


def fetch(early, pairs, sems):
    down = chosen(early)

    @pl.when(down)
    def _():
        for n, (first, _, target) in enumerate(pairs):
            pltpu.make_async_copy(first, target, sems.at[n]).start()

    @pl.when(jnp.logical_not(down))
    def _():
        for n, (_, second, target) in enumerate(pairs):
            pltpu.make_async_copy(second, target, sems.at[n]).start()


def normalise(v, gain, rows, extra):
    me = lax.axis_index("tensor")
    lane = lax.broadcasted_iota(jnp.int32, (1, 128), 1)
    for start in range(0, v.shape[0], SHARE):
        half, share = divmod(start // SHARE, TENSOR)
        part = v[start : start + SHARE]
        place = half * TENSOR + lax.bitwise_xor(me, share)
        at = pl.ds(pl.multiple_of(place * SHARE, SHARE), SHARE)
        rows[at, :] = (part * gain).astype(bf16)
        total = jnp.sum(part * part, axis=1, keepdims=True)
        high = total.astype(bf16).astype(f32)
        extra[at, :] = jnp.where(lane < 64, high, total - high).astype(bf16)


def share_products(rows, extra, weights, outs, wait=None):
    width = weights[0].shape[1]
    starts = [
        (half * TENSOR + k) * SHARE
        for half in range(len(outs) // TENSOR)
        for k in (0,) + TENSOR_ORDER
    ]
    outs = tuple(zip(starts, outs))
    for start, out in outs:
        out[:, pl.ds(2 * width, 128)] = extra[pl.ds(start, SHARE), :]
    for part, w in enumerate(weights):
        if wait is not None:
            wait(part)
        product = jnp.dot(rows[...], w[...], preferred_element_type=f32).astype(bf16)
        for start, out in outs:
            out[:, pl.ds(part * width, width)] = product[start : start + SHARE]


def enter(inputs, gains, gates, ups):
    batches, tokens, depth = inputs[0].shape
    width = gates[0].shape[2]
    total, per_data = batches * tokens, tokens // 16
    chunk = total // (CORE * X)

    def kernel(di, ui, gd, gu, dg, ug, du, uu, *refs):
        own, *others, res, wg, wu, xin, xf, xr, rows, extra, sems = refs
        outs = (own.at[pl.ds(0, SHARE)], *others[: TENSOR - 1])
        outs += (own.at[pl.ds(SHARE, SHARE)], *others[TENSOR - 1 :])
        fetch(True, ((di, ui, xin), (dg.at[0], ug.at[0], wg), (du.at[0], uu.at[0], wu)), sems)
        gain = jnp.where(chosen(True), gd[...].astype(f32), gu[...].astype(f32))
        pltpu.make_async_copy(di, xin, sems.at[0]).wait()
        for batch in range(batches):
            xf[pl.ds(batch * tokens, tokens), :] = xin[batch].astype(f32)
        dp = lax.axis_index("dp")
        x_at, core_at = dp // (ZL * CORE), lax.rem(dp, CORE)
        for c in range(CORE):
            core = core_at if c == 0 else 1 - core_at
            for j in range(X):
                group = lax.bitwise_xor(x_at, X_ORDER[j]) * (ZL * CORE) + core
                for zl in range(ZL):
                    for batch in range(batches):
                        source = pl.multiple_of(batch * tokens + (group + zl * CORE) * per_data, per_data)
                        target = (((c * X + j) * ZL + zl) * batches + batch) * per_data
                        xr[pl.ds(target, per_data), :] = xf[pl.ds(source, per_data), :]
        normalise(xr[...], gain, rows, extra)
        res[...] = xr[pl.ds(X * chunk, chunk), :].astype(bf16)

        def wait(part):
            pltpu.make_async_copy((dg, du)[part].at[0], (wg, wu)[part], sems.at[1 + part]).wait()

        share_products(rows, extra, (wg, wu), outs, wait)

    return call(
        kernel,
        [((CORE * SHARE, 2 * width + 128), bf16)]
        + [((SHARE, 2 * width + 128), bf16)] * (CORE * (TENSOR - 1))
        + [((chunk, depth), bf16)],
        [H] * 2 + [V] * 2 + [H] * 4,
        [
            pltpu.VMEM((depth, width), bf16),
            pltpu.VMEM((depth, width), bf16),
            pltpu.VMEM((batches, tokens, depth), bf16),
            pltpu.VMEM((total, depth), f32),
            pltpu.VMEM((total, depth), f32),
            pltpu.VMEM((total, depth), bf16),
            pltpu.VMEM((total, 128), bf16),
            pltpu.SemaphoreType.DMA((3,)),
        ],
        flops=4 * total * depth * width,
        moved=6 * depth * width,
        grant=ENTER_LIMIT,
    )(*inputs, *gains, *gates, *ups)


def gate_up(x, gains, gates, ups, early, after=()):
    tokens = x.shape[0]
    depth, width = gates[0].shape[1:]

    def kernel(x, gd, gu, dg, ug, du, uu, *refs):
        outs, (rows, extra) = refs[len(after) : len(after) + TENSOR], refs[len(after) + TENSOR :]
        down = chosen(early)
        gain = jnp.where(down, gd[...].astype(f32), gu[...].astype(f32))
        normalise(x[...].astype(f32), gain, rows, extra)

        @pl.when(down)
        def _():
            share_products(rows, extra, (dg.at[0], du.at[0]), outs)

        @pl.when(jnp.logical_not(down))
        def _():
            share_products(rows, extra, (ug.at[0], uu.at[0]), outs)

    return call(
        kernel,
        [((SHARE, 2 * width + 128), bf16)] * TENSOR,
        [V] * 7 + [A] * len(after),
        [pltpu.VMEM((tokens, depth), bf16), pltpu.VMEM((tokens, 128), bf16)],
        flops=4 * tokens * depth * width,
        moved=4 * depth * width,
    )(x, *gains, *gates, *ups, *after)


def hidden_of(parts, features, after=(), row=0):
    count, width = parts[1].shape[0], (parts[0].shape[1] - 128) // 2

    def kernel(a, b, c, d, *outs):
        refs, outs = (a.at[pl.ds(row, count)], b, c, d), outs[len(after) :]
        tail = sum(r[:, pl.ds(2 * width, 128)].astype(f32) for r in refs)
        squares = tail[:, 0:1] + tail[:, 64:65]
        inverse = lax.rsqrt(squares / features + EPSILON)
        gate = sum(r[:, pl.ds(0, width)].astype(f32) for r in refs) * inverse
        up = sum(r[:, pl.ds(width, width)].astype(f32) for r in refs) * inverse
        value = (gate / (1.0 + jnp.exp(-gate)) * up).astype(bf16)
        for out in outs:
            out[...] = value

    return call(kernel, [((count, width), bf16)] * TENSOR, [V] * 4 + [A] * len(after), moved=8 * count * width)(*parts, *after)


def down_part(hidden, projs, early, dtype, after=(), weight=1):
    width = hidden[0].shape[1]
    columns = projs[0].shape[2]
    half = SHARE * TENSOR

    def kernel(h0, h1, h2, h3, first, second, *refs):
        out, rows = refs[len(after) :]
        me = lax.axis_index("tensor")
        for k, share in zip((0,) + TENSOR_ORDER, (h0, h1, h2, h3)):
            at = pl.multiple_of(lax.bitwise_xor(me, k) * SHARE, SHARE)
            rows[pl.ds(at, SHARE), :] = share[...]
        down = chosen(early)

        @pl.when(down)
        def _():
            out[...] = jnp.dot(rows[...], first[0], preferred_element_type=f32).astype(dtype)

        @pl.when(jnp.logical_not(down))
        def _():
            out[...] = jnp.dot(rows[...], second[0], preferred_element_type=f32).astype(dtype)

    return call(
        kernel,
        [((half, columns), dtype)],
        [V] * 6 + [A] * len(after),
        [pltpu.VMEM((half, width), bf16)],
        flops=2 * half * width * columns * weight,
        moved=2 * width * columns * weight,
    )(*hidden, *projs, *after)[0]


def add_and_split(keep, received):
    rows, columns = keep.shape
    chunk = rows // X

    def kernel(a, b, own, s1, s2, s3):
        own[...] = a[pl.ds(0, chunk), :] + b[pl.ds(0, chunk), :].astype(f32)
        for k, out in ((1, s1), (2, s2), (3, s3)):
            at = pl.ds(k * chunk, chunk)
            out[...] = (a[at, :] + b[at, :].astype(f32)).astype(bf16)

    return call(
        kernel, [((chunk, columns), f32)] + [((chunk, columns), bf16)] * 3, [V] * 2, moved=6 * rows * columns
    )(keep, received)


def partial_sum(own, received, residual, stored=None):
    def total(a, r1, r2, r3, x):
        zl = lax.rem(lax.axis_index("dp") // CORE, ZL)
        value = a[...] + r1[...].astype(f32) + r2[...].astype(f32) + r3[...].astype(f32)
        value = value + jnp.where(zl == 0, x[pl.ds(0, a.shape[0]), :].astype(f32), 0.0)
        return zl, value.astype(bf16)

    if stored is None:

        def kernel(a, r1, r2, r3, x, near, far, kept):
            value = total(a, r1, r2, r3, x)[1]
            near[...] = value
            far[...] = value
            kept[...] = value

        return call(kernel, [(own.shape, bf16)] * 3, [V] * 5, moved=12 * own.size)(own, *received, residual)

    count = own.shape[0] // ZL

    def last(a, r1, r2, r3, x, p1, other, keep, send, scratch):
        zl, p3 = total(a, r1, r2, r3, x)
        section = lax.axis_index("section")
        outer = jnp.logical_or(section == 0, section == 3)
        scratch[0] = jnp.where(outer, other[...], p1[...])
        scratch[1] = jnp.where(outer, p3, other[...])
        mine = pl.ds(pl.multiple_of(zl * count, count), count)
        other = pl.ds(pl.multiple_of((1 - zl) * count, count), count)
        for n in range(2):
            keep[pl.ds(n * count, count), :] = scratch[n, mine, :]
            send[pl.ds(n * count, count), :] = scratch[n, other, :]

    return call(
        last,
        [(own.shape, bf16)] * 2,
        [V] * 7,
        [pltpu.VMEM((2,) + own.shape, bf16)],
        moved=20 * own.size,
    )(own, *received, residual, *stored)


def leave(keep, received, batches):
    count, columns = keep.shape[0] // 2, keep.shape[1]
    size = count // batches

    def kernel(a, b, down, up):
        first = lax.axis_index("section") < 2
        value = a[...].astype(f32) + b[...].astype(f32)
        one, two = value[:count], value[count:]
        for out, rows in ((down, jnp.where(first, one, two)), (up, jnp.where(first, two, one))):
            for batch in range(batches):
                out[0, batch] = rows[batch * size : (batch + 1) * size].astype(bf16)

    return call(
        kernel, [((1, batches, size, columns), bf16)] * 2, [V] * 2, moved=8 * keep.size
    )(keep, received)


def pair_sum(a, b):
    def kernel(p, q, *outs):
        value = (p[...].astype(f32) + q[...].astype(f32)).astype(bf16)
        for out in outs:
            out[...] = value

    return call(kernel, [(a.shape, bf16)] * X, [V] * 2, moved=6 * a.size)(a, b)


def local(
    down_input, up_input, down_gain, down_gate, down_up, down_proj, up_gain, up_gate, up_up, up_proj
):
    features = down_input.shape[2] * TENSOR
    gains = (down_gain, up_gain)
    gates, ups, projs = (down_gate, up_gate), (down_up, up_up), (down_proj, up_proj)
    stored = []
    for tick in range(4):
        early = tick < 2
        if tick == 0:
            own, *others, residual = enter((down_input, up_input), gains, gates, ups)
            parts = [own, *others[: TENSOR - 1], own, *others[TENSOR - 1 :]]
        else:
            parts = gate_up(half, gains, gates, ups, early)
            parts = parts + gate_up(rest, gains, gates, ups, early, parts[:1])
        after = parts[TENSOR : TENSOR + 1] if tick else ()
        lent = hidden_of(exchanged(parts[:TENSOR]), features, after)
        kept = hidden_of(exchanged(parts[TENSOR:]), features, lent[:1], 0 if tick else SHARE)
        made = kept[0]
        lent, kept = exchanged(lent), exchanged(kept)
        lent = down_part(lent, projs, early, bf16, (made,))
        kept = down_part(kept, projs, early, f32, (lent,), WEIGHT)
        own, *sends = add_and_split(kept, along(lent, "dp", CORE_PAIRS))
        received = [along(s, "dp", x_pairs(k)) for k, s in zip(X_ORDER[1:], sends)]
        if tick == 3:
            outer = (lax.axis_index("section") % 3) == 0
            crossed = along(jnp.where(outer, stored[0], stored[2]), "dp", CORE_PAIRS)
            keep, send = partial_sum(own, received, residual, (stored[1], crossed))
            return leave(keep, along(send, "dp", ZL_PAIRS), down_input.shape[0])
        near, far, kept = partial_sum(own, received, residual)
        stored.append(kept)
        near = along(near, ("dp", "section"), section_pairs(MOVES[tick], 0))
        far = along(far, ("dp", "section"), section_pairs(MOVES[tick], 2))
        chunk, *copies = pair_sum(near, far)
        half = [chunk] + [along(c, "dp", x_pairs(k)) for k, c in zip(X_ORDER[1:], copies)]
        half = jnp.concatenate(half, axis=0)
        residual = rest = along(half, "dp", CORE_PAIRS)


def solution(mesh):
    placed = (
        P(None, None, "tensor"),
        P(None, None, "tensor"),
        P("section", "tensor"),
        P("section", "tensor", "dp"),
        P("section", "tensor", "dp"),
        P("section", "dp", "tensor"),
        P("section", "tensor"),
        P("section", "tensor", "dp"),
        P("section", "tensor", "dp"),
        P("section", "dp", "tensor"),
    )
    return jax.shard_map(
        local,
        mesh=mesh,
        in_specs=placed,
        out_specs=(P("section", None, "dp", "tensor"), P("section", None, "dp", "tensor")),
        check_vma=False,
    )
```
